256 devices in a mesh: expert: 2 (over core), group: 64 (over z, y, x_hi), seq: 2 (over x_lo).
Axes of the slice: x: 4 (x_hi: 2, x_lo: 2; x = x_hi * 2 + x_lo), y: 4, z: 8, core: 2. Of those that a mesh axis runs over, the one named last changes fastest.
Arguments:
- latents: bfloat16 [64, 64, 256], P('group', None, 'seq'), may hold values from -6 to 6
- timestep: int32 [64], replicated, may hold values from 0 to 1023
- boundary: int32 [1], replicated, may hold values from 256 to 767
- order: int32 [64], replicated, may hold values from 0 to 63, each once
- lengths: int32 [64], replicated, may hold values from 128 to 256, as said below
- embed_weight: bfloat16 [2, 64, 5120], P('expert'), may hold values from -0.75 to 0.75
- mod_table: float32 [2, 1024, 2, 5120], P('expert', None, None, ('group', 'seq')), may hold values from -3 to 3
- qkv_weight: bfloat16 [2, 5120, 3, 3072], P('expert', None, None, 'seq'), may hold values from -0.078125 to 0.078125
- qk_gain: float32 [2, 2, 3072], P('expert', None, 'seq')
Outputs:
- attended: bfloat16 [128, 256, 3072], P(('expert', 'group'), 'seq')
The draws below stay inside these ranges and needn't reach their ends.
Inputs may be any that keep to these rules, and one draw needn't show every extreme that they name: `lengths`: the largest value is 256. `order`: each group number appears once.
All inputs are finite; a program needn't handle non-finite values.
Results may differ from the reference program's by a relative error of at most 0.01.
The reference program's roundings to bfloat16 on the way (of `normed` and `weights`) count: a program that leaves them out, or rounds other values in their place, can miss the bound.
Values may be sent and summed in bfloat16 or wider, within the bound.
A program may use at most 256 MiB of HBM per device.

```python
import jax
import jax.numpy as jnp
from jax import lax

D = 5120
HD = 128
PATCH = 64
EXPERTS = 2
HEADS = 24
NT = 1024
LEN = 256
REQS = 64
SLOTS = 128
HN = 3072
N_GROUP = 64


def draw_lengths(key, part):
    key = jax.random.fold_in(key, 11)
    first, second = jax.random.split(key)
    drawn = jax.random.randint(first, (REQS,), LEN // 2, LEN + 1)
    longest = jax.random.randint(second, (), 0, REQS)
    return jnp.where(jnp.arange(REQS) == longest, LEN, drawn).astype(jnp.int32)


def draw_qk_gain(key, part):
    key = jax.random.fold_in(key, 7)
    first = jax.random.fold_in(key, 0)
    base = jnp.exp(jax.random.uniform(first, (EXPERTS, 2, HEADS * HD), jnp.float32, 0.0, jnp.log(2.5)))
    ramp = 3.0 ** (0.5 * jnp.arange(HEADS * HD, dtype=jnp.float32) / (HEADS * HD - 1))
    gain = base * ramp
    return gain.astype(jnp.float32)


def set_ends(result, stream_key, least, top_value):
    extent = result.shape
    place = [jax.random.randint(jax.random.fold_in(stream_key, axis), (), 0, extent[axis]) for axis in range(len(extent))]
    result = result.at[tuple(place)].set(least)
    longest = extent.index(max(extent))
    place[longest] = (place[longest] + 1) % extent[longest]
    return result.at[tuple(place)].set(top_value)


def block_levels(rng, shape, cuts, least, high):
    level = 1.0
    for dim, parts in cuts:
        draws = jax.random.uniform(jax.random.fold_in(jax.random.fold_in(rng, 6), dim), (parts,), jnp.float32, least / len(cuts), high / len(cuts))
        level = level * jnp.repeat(jnp.exp(draws), shape[dim] // parts).reshape((-1,) + (1,) * (len(shape) - 1 - dim))
    return level


def bell_draw(own_key, extent, spread, reach, shards=(), held_as=jnp.bfloat16):
    loudness = block_levels(own_key, extent, shards, -0.22, 0.18) if shards else 1.0
    values = jax.random.normal(own_key, extent, jnp.float32) * spread * loudness
    return jnp.minimum(jnp.maximum(values, -reach), reach).astype(held_as)


def setup_inputs(seed: int = 0) -> dict:
    key_list = jax.random.split(jax.random.key(seed), 10)
    latents = bell_draw(key_list[0], (REQS, PATCH, LEN), 1.0, 6.0, ((0, 64), (2, 2)))
    timestep = set_ends(jax.random.randint(key_list[1], (REQS,), 0, NT), jax.random.fold_in(key_list[1], 1), 0, NT - 1).astype(jnp.int32)
    boundary = jax.random.randint(key_list[2], (1,), NT // 4, 3 * NT // 4).astype(jnp.int32)
    order = jax.random.permutation(key_list[3], REQS).astype(jnp.int32)
    lengths = draw_lengths(jax.random.fold_in(key_list[9], 71), 0)
    embed_weight = bell_draw(key_list[5], (EXPERTS, PATCH, D), PATCH ** -0.5, 0.75, ((0, 2),))
    mod_table = bell_draw(key_list[6], (EXPERTS, NT, 2, D), 0.5, 3.0, ((0, 2), (3, 128)), jnp.float32)
    qkv_weight = bell_draw(key_list[7], (EXPERTS, D, 3, HN), D ** -0.5, 0.078125, ((0, 2), (3, 2)))
    qk_gain = draw_qk_gain(jax.random.fold_in(key_list[9], 71), 0)
    return dict(latents=latents, timestep=timestep, boundary=boundary, order=order, lengths=lengths, embed_weight=embed_weight, mod_table=mod_table, qkv_weight=qkv_weight, qk_gain=qk_gain)


def one_request(index, latents, timestep, expert_of, lengths, embed_weight, mod_table, qkv_weight, qk_gain):
    which = expert_of[index]
    patches = latents[index]
    embedded = jnp.dot(patches.T, embed_weight[which], preferred_element_type=jnp.float32)
    coeffs = mod_table[which, timestep[index]]
    mean = lax.optimization_barrier(jnp.mean(embedded, axis=1, keepdims=True))
    centred = embedded - mean
    var = lax.optimization_barrier(jnp.mean(centred * centred, axis=1, keepdims=True))
    normed = (centred / jnp.sqrt(var + 1e-06) * (1.0 + coeffs[1]) + coeffs[0]).astype(jnp.bfloat16)
    weights = qkv_weight[which].reshape(D, 3 * HN)
    projected = jnp.dot(normed, weights, preferred_element_type=jnp.float32)
    query = projected[:, :HN]
    key = projected[:, HN:2 * HN]
    value = projected[:, 2 * HN:].astype(jnp.bfloat16)
    gains = qk_gain[which]
    query_n = (query / jnp.sqrt(lax.optimization_barrier(jnp.mean(query * query, axis=1, keepdims=True)) + 1e-06) * gains[0]).astype(jnp.bfloat16)
    key_n = (key / jnp.sqrt(lax.optimization_barrier(jnp.mean(key * key, axis=1, keepdims=True)) + 1e-06) * gains[1]).astype(jnp.bfloat16)
    queries = query_n.reshape(LEN, HEADS, HD).astype(jnp.float32)
    keys = key_n.reshape(LEN, HEADS, HD).astype(jnp.float32)
    values = value.reshape(LEN, HEADS, HD).astype(jnp.float32)
    scores = jnp.einsum('qhd,khd->hqk', queries, keys) * HD ** (-0.5)
    positions = jnp.arange(LEN, dtype=jnp.int32)
    live = positions < lengths[index]
    scores = jnp.where(live[None, None, :], scores, -jnp.inf)
    top = lax.optimization_barrier(jnp.max(scores, axis=2, keepdims=True))
    expd = jnp.exp(scores - top)
    probs = (expd / lax.optimization_barrier(jnp.sum(expd, axis=2, keepdims=True))).astype(jnp.bfloat16)
    mixed = jnp.einsum('hqk,khd->qhd', probs.astype(jnp.float32), values)
    mixed = jnp.where(live[:, None, None], mixed, 0.0)
    return mixed.reshape(LEN, HN).astype(jnp.bfloat16)

def reference(latents, timestep, boundary, order, lengths, embed_weight, mod_table, qkv_weight, qk_gain):
    expert_of = jnp.where(timestep >= boundary[0], 0, 1).astype(jnp.int32)
    slot_of = (expert_of * N_GROUP + order).astype(jnp.int32)

    def run(index):
        return one_request(index, latents, timestep, expert_of, lengths, embed_weight, mod_table, qkv_weight, qk_gain)
    results = lax.map(run, jnp.arange(REQS, dtype=jnp.int32))
    attended = jnp.zeros((SLOTS, LEN, HN), jnp.bfloat16)
    return attended.at[slot_of].set(results)
```

```python
import jax
import jax.numpy as jnp
from jax import lax
from jax.experimental import pallas as pl
from jax.experimental.pallas import tpu as pltpu
from jax.sharding import PartitionSpec as P

HD = 128
EPS = 1e-06
MESH = pl.DeviceIdType.MESH
F32 = jnp.float32
BF16 = jnp.bfloat16
NZ = 8
ND = 8
CW = 256
HI = lax.Precision.HIGHEST


def kernel(
    order_s, time_s, bound_s, len_s, lat_ref, gain_ref, emb_hbm, tab_hbm, w_hbm,
    out_hbm,
    emb_v, tab_v, wbuf,
    lat_all, lat_send, lat_recv, mod_src, mod_all, mod_send, mod_recv, mod_row,
    xt, normed, proj, vbuf, kbuf, sq_send, sq_recv, out_far, out_own,
    loc_sem, w_sem, l1_send, l1_recv, m1_send, m1_recv, l2_send, l2_recv, m2_send, m2_recv,
    sq_sem, o_send, o_recv,
):
    g = lax.axis_index("group")
    s = lax.axis_index("seq")
    e = lax.axis_index("expert")
    z = g // ND
    d = g % ND
    p = d * 2 + s
    reqs = NZ * ND
    tokens = 256
    half = 128
    feats = emb_v.shape[1]
    chunks = w_hbm.shape[2] // CW
    width = w_hbm.shape[2]

    emb_cp = pltpu.make_async_copy(emb_hbm.at[0], emb_v, loc_sem.at[0])
    tab_cp = pltpu.make_async_copy(tab_hbm, tab_v, loc_sem.at[1])
    tab_cp.start()
    emb_cp.start()

    def w_copy(i):
        return pltpu.make_async_copy(
            w_hbm.at[i // chunks, :, pl.ds(pl.multiple_of((i % chunks) * CW, CW), CW)],
            wbuf.at[i], w_sem.at[i],
        )

    barrier = pltpu.get_barrier_semaphore()

    def greet_z(k, c):
        pl.semaphore_signal(barrier, inc=1, device_id={"group": ((z + k) % NZ) * ND + d}, device_id_type=MESH)
        return c

    def greet_p(k, c):
        q = (p + k) % (2 * ND)
        pl.semaphore_signal(barrier, inc=1, device_id={"group": z * ND + q // 2, "seq": q % 2}, device_id_type=MESH)
        return c

    lax.fori_loop(1, NZ, greet_z, 0)
    lax.fori_loop(1, 2 * ND, greet_p, 0)
    pl.semaphore_wait(barrier, NZ - 1 + 2 * ND - 1)

    def l1_copy(k, slot):
        return pltpu.make_async_remote_copy(
            src_ref=lat_ref.at[0], dst_ref=lat_all.at[slot], send_sem=l1_send.at[k], recv_sem=l1_recv.at[slot],
            device_id={"group": ((z + k) % NZ) * ND + d}, device_id_type=MESH)

    def l1_start(k, c):
        l1_copy(k, z).start()
        return c

    lax.fori_loop(1, NZ, l1_start, 0)
    lat_all[z] = lat_ref[0]

    def w_start(i, c):
        w_copy(i).start()
        return c

    lax.fori_loop(0, 3 * chunks, w_start, 0)

    rows = lax.broadcasted_iota(jnp.int32, (reqs, 128), 0)

    def pick(r, c):
        col, stamp, live = c
        where = order_s[r]
        col = jnp.where(rows == where, time_s[r], col)
        mine = where == g
        return col, jnp.where(mine, time_s[r], stamp), jnp.where(mine, len_s[r], live)

    col, stamp, live = lax.fori_loop(
        0, reqs, pick, (jnp.zeros((reqs, 128), jnp.int32), jnp.int32(0), jnp.int32(0)), unroll=8)
    expert_of = jnp.where(stamp >= bound_s[0], 0, 1)
    shown = jnp.where(expert_of == e, live, 0)

    steps = tab_v.shape[1]
    tab_cp.wait()
    hit = (lax.broadcasted_iota(jnp.int32, (reqs, steps), 1) == col[:, :1]).astype(F32)
    picked = lax.dot_general(hit, tab_v[...], (((1,), (1,)), ((), ())), precision=HI, preferred_element_type=F32)
    mod_src[...] = jnp.zeros_like(mod_src)
    for a in range(NZ):
        mod_src[a, :, : tab_v.shape[0]] = picked[a * ND : (a + 1) * ND]

    def m1_copy(k, slot):
        z2 = (z + k) % NZ
        return pltpu.make_async_remote_copy(
            src_ref=mod_src.at[z2], dst_ref=mod_all.at[slot], send_sem=m1_send.at[k], recv_sem=m1_recv.at[slot],
            device_id={"group": z2 * ND + d}, device_id_type=MESH)

    def m1_start(k, c):
        m1_copy(k, z).start()
        return c

    lax.fori_loop(1, NZ, m1_start, 0)
    mod_all[z] = mod_src[z]

    def l1_wait(k, c):
        l1_copy(k, (z + k) % NZ).wait_recv()
        return c

    lax.fori_loop(1, NZ, l1_wait, 0)
    for b in range(ND):
        chosen = jnp.zeros(lat_all.shape[1:], BF16)
        for a in range(NZ):
            chosen = jnp.where(order_s[a * ND + d] == z * ND + b, lat_all[a], chosen)
        lat_send[b] = chosen

    def l2_copy(k, slot):
        q = (p + k) % (2 * ND)
        return pltpu.make_async_remote_copy(
            src_ref=lat_send.at[q // 2], dst_ref=lat_recv.at[slot], send_sem=l2_send.at[k], recv_sem=l2_recv.at[slot],
            device_id={"group": z * ND + q // 2, "seq": q % 2}, device_id_type=MESH)

    def l2_start(k, c):
        l2_copy(k, p).start()
        return c

    lax.fori_loop(1, 2 * ND, l2_start, 0)
    lat_recv[p] = lat_send[d]

    def m1_wait(k, c):
        m1_copy(k, (z + k) % NZ).wait_recv()
        return c

    lax.fori_loop(1, NZ, m1_wait, 0)
    for b in range(ND):
        for a in range(NZ):
            mod_send[b, a : a + 1] = mod_all[a, b : b + 1]

    def m2_copy(k, slot):
        q = (p + k) % (2 * ND)
        return pltpu.make_async_remote_copy(
            src_ref=mod_send.at[q // 2], dst_ref=mod_recv.at[slot], send_sem=m2_send.at[k], recv_sem=m2_recv.at[slot],
            device_id={"group": z * ND + q // 2, "seq": q % 2}, device_id_type=MESH)

    def m2_start(k, c):
        m2_copy(k, p).start()
        return c

    lax.fori_loop(1, 2 * ND, m2_start, 0)
    mod_recv[p] = mod_send[d]

    emb_cp.wait()
    wbar = jnp.sum(emb_v[...].astype(F32), axis=1, keepdims=True) * (1.0 / feats)
    wbar = jnp.broadcast_to(wbar, (wbar.shape[0], 128))

    def l2_wait(k, c):
        l2_copy(k, (p + k) % (2 * ND)).wait_recv()
        return c

    lax.fori_loop(1, 2 * ND, l2_wait, 0)
    for t in range(2):
        x = lat_recv[t].astype(F32)
        for b in range(1, ND):
            x = x + lat_recv[2 * b + t].astype(F32)
        xt[t * half : (t + 1) * half] = jnp.transpose(x).astype(BF16)

    mean = lax.dot_general(xt[...].astype(F32), wbar, (((1,), (0,)), ((), ())), precision=HI, preferred_element_type=F32)
    et = 256
    tiles = feats // et

    def embed(t, i):
        cols = pl.ds(pl.multiple_of(i * et, et), et)
        made = jnp.dot(xt[t * half : (t + 1) * half], emb_v[:, cols], preferred_element_type=F32)
        m = mean[t * half : (t + 1) * half, :1]
        return made - m

    def spread(t):
        def body(i, ss):
            c = embed(t, i)
            c = c * c
            return ss + c[:, :128] + c[:, 128:]
        ss = lax.fori_loop(0, tiles, body, jnp.zeros((half, 128), F32))
        var = jnp.sum(ss, axis=1, keepdims=True) * (1.0 / feats)
        return 1.0 / jnp.sqrt(var + EPS)

    rstd = [spread(t) for t in range(2)]

    def m2_wait(k, c):
        m2_copy(k, (p + k) % (2 * ND)).wait_recv()
        return c

    lax.fori_loop(1, 2 * ND, m2_wait, 0)
    own = tab_v.shape[0] // 2
    lane = lax.broadcasted_iota(jnp.int32, (NZ, 128), 1)
    span = 2 * ND * own // 128
    for c in range(2):
        pieces = [jnp.zeros((NZ, 128), F32) for _ in range(span)]
        for q in range(2 * ND):
            start = q * own
            off = start % 128
            turned = pltpu.roll(mod_recv[q], (off - c * own) % 128, 1)
            a = start // 128
            pieces[a] = jnp.where((lane >= off) & (lane < off + own), turned, pieces[a])
            if off + own > 128:
                pieces[a + 1] = jnp.where(lane < off + own - 128, turned, pieces[a + 1])
        for a in range(span):
            for b in range(NZ):
                n = (b * span + a) * 128
                mod_row[c : c + 1, n : n + 128] = pieces[a][b : b + 1] + float(c)

    for t in range(2):
        def body(i, c, t=t):
            cols = pl.ds(pl.multiple_of(i * et, et), et)
            v = embed(t, i) * rstd[t] * mod_row[1:2, cols] + mod_row[0:1, cols]
            normed[t * half : (t + 1) * half, cols] = v.astype(BF16)
            return c
        lax.fori_loop(0, tiles, body, 0)

    def project(i):
        w_copy(i).wait()
        return jnp.dot(normed[...], wbuf[i], preferred_element_type=F32)

    def squares(base):
        def body(i, ss):
            made = project(base + i)
            proj[base + i] = made
            made = made * made
            return ss + made[:, :128] + made[:, 128:]
        ss = lax.fori_loop(0, chunks, body, jnp.zeros((tokens, 128), F32))
        return jnp.sum(ss, axis=1, keepdims=True)

    q_ss = squares(0)
    k_ss = squares(chunks)
    lane_t = lax.broadcasted_iota(jnp.int32, (tokens, 128), 1)
    sq_send[...] = jnp.where(lane_t < 64, q_ss, k_ss)
    sq_cp = pltpu.make_async_remote_copy(
        src_ref=sq_send, dst_ref=sq_recv, send_sem=sq_sem.at[0], recv_sem=sq_sem.at[1],
        device_id={"seq": 1 - s}, device_id_type=MESH)
    sq_cp.start()

    def values(i, c):
        vbuf[i] = project(2 * chunks + i).astype(BF16)
        return c

    lax.fori_loop(0, chunks, values, 0)
    sq_cp.wait_recv()
    total = sq_send[...] + sq_recv[...]
    inv = 1.0 / jnp.sqrt(total * (1.0 / (2 * width)) + EPS)
    sq_send_done = sq_cp.wait_send
    sq_send_done()
    sq_send[...] = inv

    keypos = lax.broadcasted_iota(jnp.int32, (half, tokens), 1)
    rowpos = lax.broadcasted_iota(jnp.int32, (half, HD), 0)

    def attend(i, r0, out_ref, first):
        cols = pl.ds(pl.multiple_of(i * CW, CW), CW)
        gq = gain_ref[0, 0:1, cols]
        at = pl.ds(pl.multiple_of(r0, half), half)
        if first:
            gk = gain_ref[0, 1:2, cols]
            kbuf[i] = (proj[chunks + i] * sq_send[:, 64:65] * gk).astype(BF16)
        q2 = (proj[i, at, :] * sq_send[at, 0:1] * gq).astype(BF16)
        for j in range(CW // HD):
            hc = slice(j * HD, (j + 1) * HD)
            sc = lax.dot_general(q2[:, hc], kbuf[i, :, hc], (((1,), (1,)), ((), ())), preferred_element_type=F32)
            sc = jnp.where(keypos < live, sc * HD ** (-0.5), -jnp.inf)
            ex = jnp.exp(sc - jnp.max(sc, axis=1, keepdims=True))
            pr = (ex * (1.0 / jnp.sum(ex, axis=1, keepdims=True))).astype(BF16)
            mixed = jnp.dot(pr, vbuf[i, :, hc], preferred_element_type=F32)
            mixed = jnp.where(rowpos + r0 < shown, mixed, 0.0)
            out_ref[:, pl.ds(pl.multiple_of(i * CW + j * HD, HD), HD)] = mixed.astype(BF16)

    def o_copy(i, side):
        cols = pl.ds(pl.multiple_of(i * CW, CW), CW)
        there = pl.ds(pl.multiple_of(side * width + i * CW, CW), CW)
        return pltpu.make_async_remote_copy(
            src_ref=out_far.at[:, cols], dst_ref=out_hbm.at[0, :, there], send_sem=o_send.at[i], recv_sem=o_recv.at[i],
            device_id={"seq": 1 - s}, device_id_type=MESH)

    def far(i, c):
        attend(i, (1 - s) * half, out_far, True)
        o_copy(i, s).start()
        return c

    lax.fori_loop(0, chunks, far, 0)

    def near(i, c):
        attend(i, s * half, out_own, False)
        return c

    lax.fori_loop(0, chunks, near, 0)
    own_cp = pltpu.make_async_copy(
        out_own, out_hbm.at[0, :, pl.ds(pl.multiple_of(s * width, width), width)], loc_sem.at[2])
    own_cp.start()

    def sends_z(k, c):
        l1_copy(k, z).wait_send()
        m1_copy(k, z).wait_send()
        return c

    def sends_p(k, c):
        l2_copy(k, p).wait_send()
        m2_copy(k, p).wait_send()
        return c

    lax.fori_loop(1, NZ, sends_z, 0)
    lax.fori_loop(1, 2 * ND, sends_p, 0)

    def o_wait(i, c):
        o_copy(i, 1 - s).wait_recv()
        o_copy(i, s).wait_send()
        return c

    lax.fori_loop(0, chunks, o_wait, 0)
    own_cp.wait()


def per_device(latents, timestep, boundary, order, lengths, embed_weight, mod_table, qkv_weight, qk_gain):
    patch, feats = embed_weight.shape[1:]
    width = qkv_weight.shape[3]
    chunks = width // CW
    steps = mod_table.shape[1]
    table = jnp.transpose(mod_table[0], (1, 2, 0)).reshape(-1, steps)
    weights = jnp.transpose(qkv_weight[0], (1, 0, 2))
    tokens, half = 256, 128
    smem = pl.BlockSpec(memory_space=pltpu.SMEM)
    vmem = pl.BlockSpec(memory_space=pltpu.VMEM)
    anywhere = pl.BlockSpec(memory_space=pl.ANY)
    dma = pltpu.SemaphoreType.DMA
    return pl.pallas_call(
        kernel,
        out_shape=jax.ShapeDtypeStruct((1, half, 2 * width), BF16),
        in_specs=[smem] * 4 + [vmem] * 2 + [anywhere] * 3,
        out_specs=anywhere,
        scratch_shapes=[
            pltpu.VMEM((patch, feats), BF16),
            pltpu.VMEM(table.shape, F32),
            pltpu.VMEM((3 * chunks, feats, CW), BF16),
            pltpu.VMEM((NZ, patch, half), BF16),
            pltpu.VMEM((ND, patch, half), BF16),
            pltpu.VMEM((2 * ND, patch, half), BF16),
            pltpu.VMEM((NZ, ND, 128), F32),
            pltpu.VMEM((NZ, ND, 128), F32),
            pltpu.VMEM((ND, NZ, 128), F32),
            pltpu.VMEM((2 * ND, NZ, 128), F32),
            pltpu.VMEM((2, feats), F32),
            pltpu.VMEM((tokens, patch), BF16),
            pltpu.VMEM((tokens, feats), BF16),
            pltpu.VMEM((2 * chunks, tokens, CW), F32),
            pltpu.VMEM((chunks, tokens, CW), BF16),
            pltpu.VMEM((chunks, tokens, CW), BF16),
            pltpu.VMEM((tokens, 128), F32),
            pltpu.VMEM((tokens, 128), F32),
            pltpu.VMEM((half, width), BF16),
            pltpu.VMEM((half, width), BF16),
            dma((3,)),
            dma((3 * chunks,)),
            dma((NZ,)), dma((NZ,)), dma((NZ,)), dma((NZ,)),
            dma((2 * ND,)), dma((2 * ND,)), dma((2 * ND,)), dma((2 * ND,)),
            dma((2,)),
            dma((chunks,)), dma((chunks,)),
        ],
        compiler_params=pltpu.CompilerParams(
            collective_id=0, has_side_effects=True, vmem_limit_bytes=62 * 1024 * 1024),
        cost_estimate=pl.CostEstimate(flops=13 * 10**9, bytes_accessed=49 * 10**6, transcendentals=800000),
    )(order, timestep, boundary, lengths, latents, qk_gain, embed_weight, table, weights)


def solution(mesh):
    in_specs = (
        P("group", None, "seq"),
        P(),
        P(),
        P(),
        P(),
        P("expert", None, None),
        P("expert", None, None, ("group", "seq")),
        P("expert", None, None, "seq"),
        P("expert", None, "seq"),
    )
    out_specs = P(("expert", "group"), "seq", None)
    return jax.shard_map(
        per_device, mesh=mesh, in_specs=in_specs, out_specs=out_specs, check_vma=False
    )
```

```python
import jax
import jax.numpy as jnp
from jax import lax
from jax.experimental import pallas as pl
from jax.experimental.pallas import tpu as pltpu
from jax.sharding import PartitionSpec as P

HD = 128
EPS = 1e-06
MESH = pl.DeviceIdType.MESH
F32 = jnp.float32
BF16 = jnp.bfloat16
NZ = 8
ND = 8
CW = 256
HI = lax.Precision.HIGHEST
UNROLL = 3
PAIRS = 3


def kernel(
    order_s, time_s, bound_s, len_s, lat_ref, gain_ref, emb_hbm, tab_hbm, w_hbm,
    out_hbm,
    emb_v, tab_v, wbuf,
    lat_all, lat_send, lat_recv, mod_src, mod_all, mod_send, mod_recv, mod_row,
    xt, normed, proj, vbuf, kbuf, sq_send, sq_recv, inv_qk, out_far, out_own,
    loc_sem, w_sem, l1_send, l1_recv, m1_send, m1_recv, l2_send, l2_recv, m2_send, m2_recv,
    sq_sem, o_send, o_recv,
):
    g = lax.axis_index("group")
    s = lax.axis_index("seq")
    e = lax.axis_index("expert")
    z = g // ND
    d = g % ND
    p = d * 2 + s
    reqs = NZ * ND
    tokens = 256
    half = 128
    feats = emb_v.shape[1]
    chunks = w_hbm.shape[2] // CW
    width = w_hbm.shape[2]

    emb_cp = pltpu.make_async_copy(emb_hbm.at[0], emb_v, loc_sem.at[0])
    tab_cp = pltpu.make_async_copy(tab_hbm, tab_v, loc_sem.at[1])
    tab_cp.start()
    emb_cp.start()

    def w_copy(i):
        return pltpu.make_async_copy(
            w_hbm.at[i // chunks, :, pl.ds(pl.multiple_of((i % chunks) * CW, CW), CW)],
            wbuf.at[i], w_sem.at[i],
        )

    def w_start(i, c):
        w_copy(i).start()
        return c

    lax.fori_loop(0, 3 * chunks, w_start, 0)

    barrier = pltpu.get_barrier_semaphore()

    def greet_z(k, c):
        pl.semaphore_signal(barrier, inc=1, device_id={"group": ((z + k) % NZ) * ND + d}, device_id_type=MESH)
        return c

    def greet_p(k, c):
        q = (p + k) % (2 * ND)
        pl.semaphore_signal(barrier, inc=1, device_id={"group": z * ND + q // 2, "seq": q % 2}, device_id_type=MESH)
        return c

    lax.fori_loop(1, NZ, greet_z, 0)
    lax.fori_loop(1, 2 * ND, greet_p, 0)
    pl.semaphore_wait(barrier, NZ - 1 + 2 * ND - 1)

    def l1_copy(k, slot):
        return pltpu.make_async_remote_copy(
            src_ref=lat_ref.at[0], dst_ref=lat_all.at[slot], send_sem=l1_send.at[k], recv_sem=l1_recv.at[slot],
            device_id={"group": ((z + k) % NZ) * ND + d}, device_id_type=MESH)

    def l1_start(k, c):
        l1_copy(k, z).start()
        return c

    lax.fori_loop(1, NZ, l1_start, 0)
    lat_all[z] = lat_ref[0]

    rows = lax.broadcasted_iota(jnp.int32, (reqs, 128), 0)

    def pick(r, c):
        col, stamp, live = c
        where = order_s[r]
        col = jnp.where(rows == where, time_s[r], col)
        mine = where == g
        return col, jnp.where(mine, time_s[r], stamp), jnp.where(mine, len_s[r], live)

    col, stamp, live = lax.fori_loop(
        0, reqs, pick, (jnp.zeros((reqs, 128), jnp.int32), jnp.int32(0), jnp.int32(0)), unroll=8)
    expert_of = jnp.where(stamp >= bound_s[0], 0, 1)
    shown = jnp.where(expert_of == e, live, 0)

    steps = tab_v.shape[1]
    tab_cp.wait()
    hit = (lax.broadcasted_iota(jnp.int32, (reqs, steps), 1) == col[:, :1]).astype(F32)
    picked = lax.dot_general(hit, tab_v[...], (((1,), (1,)), ((), ())), precision=HI, preferred_element_type=F32)
    mod_src[...] = jnp.zeros_like(mod_src)
    for a in range(NZ):
        mod_src[a, :, : tab_v.shape[0]] = picked[a * ND : (a + 1) * ND]

    def m1_copy(k, slot):
        z2 = (z + k) % NZ
        return pltpu.make_async_remote_copy(
            src_ref=mod_src.at[z2], dst_ref=mod_all.at[slot], send_sem=m1_send.at[k], recv_sem=m1_recv.at[slot],
            device_id={"group": z2 * ND + d}, device_id_type=MESH)

    def m1_start(k, c):
        m1_copy(k, z).start()
        return c

    lax.fori_loop(1, NZ, m1_start, 0)
    mod_all[z] = mod_src[z]

    def l1_wait(k, c):
        l1_copy(k, (z + k) % NZ).wait_recv()
        return c

    lax.fori_loop(1, NZ, l1_wait, 0)
    for b in range(ND):
        chosen = jnp.zeros(lat_all.shape[1:], BF16)
        for a in range(NZ):
            chosen = jnp.where(order_s[a * ND + d] == z * ND + b, lat_all[a], chosen)
        lat_send[b] = chosen

    def l2_copy(k, slot):
        q = (p + k) % (2 * ND)
        return pltpu.make_async_remote_copy(
            src_ref=lat_send.at[q // 2], dst_ref=lat_recv.at[slot], send_sem=l2_send.at[k], recv_sem=l2_recv.at[slot],
            device_id={"group": z * ND + q // 2, "seq": q % 2}, device_id_type=MESH)

    def l2_start(k, c):
        l2_copy(k, p).start()
        return c

    lax.fori_loop(1, 2 * ND, l2_start, 0)
    lat_recv[p] = lat_send[d]

    def m1_wait(k, c):
        m1_copy(k, (z + k) % NZ).wait_recv()
        return c

    lax.fori_loop(1, NZ, m1_wait, 0)
    for b in range(ND):
        for a in range(NZ):
            mod_send[b, a : a + 1] = mod_all[a, b : b + 1]

    def m2_copy(k, slot):
        q = (p + k) % (2 * ND)
        return pltpu.make_async_remote_copy(
            src_ref=mod_send.at[q // 2], dst_ref=mod_recv.at[slot], send_sem=m2_send.at[k], recv_sem=m2_recv.at[slot],
            device_id={"group": z * ND + q // 2, "seq": q % 2}, device_id_type=MESH)

    def m2_start(k, c):
        m2_copy(k, p).start()
        return c

    lax.fori_loop(1, 2 * ND, m2_start, 0)
    mod_recv[p] = mod_send[d]

    emb_cp.wait()
    wbar = jnp.sum(emb_v[...].astype(F32), axis=1, keepdims=True) * (1.0 / feats)
    wbar = jnp.broadcast_to(wbar, (wbar.shape[0], 128))

    def l2_wait(k, c):
        l2_copy(k, (p + k) % (2 * ND)).wait_recv()
        return c

    lax.fori_loop(1, 2 * ND, l2_wait, 0)
    for t in range(2):
        x = lat_recv[t].astype(F32)
        for b in range(1, ND):
            x = x + lat_recv[2 * b + t].astype(F32)
        xt[t * half : (t + 1) * half] = jnp.transpose(x).astype(BF16)

    mean = lax.dot_general(xt[...].astype(F32), wbar, (((1,), (0,)), ((), ())), precision=HI, preferred_element_type=F32)
    et = 256
    tiles = feats // et
    near_each = 10

    def embed(t, n):
        made = jnp.dot(xt[t * half : (t + 1) * half], emb_v[:, pl.ds(pl.multiple_of(n * et, et), et)],
                       preferred_element_type=F32)
        m = mean[t * half : (t + 1) * half]
        return made[:, :128] - m, made[:, 128:] - m

    def spread(t):
        def body(i, ss):
            for u in range(near_each):
                c0, c1 = embed(t, i * near_each + u)
                ss = ss + (c0 * c0 + c1 * c1)
            return ss
        ss = lax.fori_loop(0, tiles // near_each, body, jnp.zeros((half, 128), F32))
        var = jnp.sum(ss, axis=1, keepdims=True) * (1.0 / feats)
        return jnp.broadcast_to(1.0 / jnp.sqrt(var + EPS), (half, 128))

    rstd = [spread(t) for t in range(2)]

    def m2_wait(k, c):
        m2_copy(k, (p + k) % (2 * ND)).wait_recv()
        return c

    lax.fori_loop(1, 2 * ND, m2_wait, 0)
    own = tab_v.shape[0] // 2
    lane = lax.broadcasted_iota(jnp.int32, (NZ, 128), 1)
    span = 2 * ND * own // 128
    for c in range(2):
        pieces = [jnp.zeros((NZ, 128), F32) for _ in range(span)]
        for q in range(2 * ND):
            start = q * own
            off = start % 128
            turned = pltpu.roll(mod_recv[q], (off - c * own) % 128, 1)
            a = start // 128
            pieces[a] = jnp.where((lane >= off) & (lane < off + own), turned, pieces[a])
            if off + own > 128:
                pieces[a + 1] = jnp.where(lane < off + own - 128, turned, pieces[a + 1])
        for a in range(span):
            for b in range(NZ):
                n = (b * span + a) * 128
                mod_row[c : c + 1, n : n + 128] = pieces[a][b : b + 1] + float(c)

    for t in range(2):
        def body(i, c, t=t):
            for u in range(near_each):
                n = i * near_each + u
                for h, v in enumerate(embed(t, n)):
                    cols = pl.ds(pl.multiple_of(n * et + h * 128, 128), 128)
                    v = v * rstd[t] * mod_row[1:2, cols] + mod_row[0:1, cols]
                    normed[t * half : (t + 1) * half, cols] = v.astype(BF16)
            return c
        lax.fori_loop(0, tiles // near_each, body, 0)

    def arrive(base):
        def body(i, c):
            w_copy(base + i).wait()
            return c
        lax.fori_loop(0, chunks, body, 0)

    def project(i):
        return jnp.dot(normed[...], wbuf[i], preferred_element_type=F32)

    def squares(base):
        def body(i, ss):
            made = project(base + i)
            proj[base + i] = made
            made = made * made
            return ss + (made[:, :128] + made[:, 128:])
        return lax.fori_loop(0, chunks, body, jnp.zeros((tokens, 128), F32), unroll=UNROLL)

    ones = jnp.ones((8, 128), F32)

    def as_rows(ss):
        return lax.dot_general(ones, ss, (((1,), (1,)), ((), ())), precision=HI, preferred_element_type=F32)

    arrive(0)
    q_ss = squares(0)
    arrive(chunks)
    k_ss = squares(chunks)
    sq_send[0] = as_rows(q_ss)
    sq_send[1] = as_rows(k_ss)
    sq_cp = pltpu.make_async_remote_copy(
        src_ref=sq_send, dst_ref=sq_recv, send_sem=sq_sem.at[0], recv_sem=sq_sem.at[1],
        device_id={"seq": 1 - s}, device_id_type=MESH)
    sq_cp.start()

    def values(i, c):
        vbuf[i] = project(2 * chunks + i).astype(BF16)
        return c

    first = chunks // 2
    arrive(2 * chunks)
    lax.fori_loop(0, first, values, 0, unroll=UNROLL)
    sq_cp.wait_recv()
    for c in range(2):
        total = sq_send[c] + sq_recv[c]
        inv = 1.0 / jnp.sqrt(total * (1.0 / (2 * width)) + EPS)
        inv = jnp.broadcast_to(inv[0:1], (128, tokens))
        inv_qk[c] = jnp.transpose(inv)

    keypos = lax.broadcasted_iota(jnp.int32, (half, tokens), 1)
    rowpos = lax.broadcasted_iota(jnp.int32, (half, HD), 0)

    def attend(i, r0, out_ref, first):
        at = pl.ds(pl.multiple_of(r0, half), half)
        work = []
        for u in range(PAIRS):
            n = i * PAIRS + u
            for j in range(CW // HD):
                hc = slice(j * HD, (j + 1) * HD)
                cols = pl.ds(pl.multiple_of(n * CW + j * HD, HD), HD)
                if first:
                    kbuf[n, :, hc] = (proj[chunks + n, :, hc] * inv_qk[1] * gain_ref[0, 1:2, cols]).astype(BF16)
                qn = (proj[n, at, hc] * inv_qk[0, at, :] * gain_ref[0, 0:1, cols]).astype(BF16)
                work.append((n, hc, cols, qn))
        scores = [lax.dot_general(qn, kbuf[n, :, hc], (((1,), (1,)), ((), ())), preferred_element_type=F32)
                  for n, hc, _, qn in work]
        parts = []
        for sc in scores:
            sc = jnp.where(keypos < live, sc * HD ** (-0.5), -jnp.inf)
            ex = jnp.exp(sc - jnp.max(sc, axis=1, keepdims=True))
            parts.append((ex * (1.0 / jnp.sum(ex, axis=1, keepdims=True))).astype(BF16))
        for (n, hc, cols, _), pr in zip(work, parts):
            mixed = jnp.dot(pr, vbuf[n, :, hc], preferred_element_type=F32)
            out_ref[:, cols] = jnp.where(rowpos + r0 < shown, mixed, 0.0).astype(BF16)

    def o_copy(i, side):
        cols = pl.ds(pl.multiple_of(i * CW, CW), CW)
        there = pl.ds(pl.multiple_of(side * width + i * CW, CW), CW)
        return pltpu.make_async_remote_copy(
            src_ref=out_far.at[:, cols], dst_ref=out_hbm.at[0, :, there], send_sem=o_send.at[i], recv_sem=o_recv.at[i],
            device_id={"seq": 1 - s}, device_id_type=MESH)

    def far(i, c):
        attend(i, (1 - s) * half, out_far, True)
        for u in range(PAIRS):
            o_copy(i * PAIRS + u, s).start()
        return c

    far(0, 0)
    lax.fori_loop(first, chunks, values, 0, unroll=UNROLL)
    far(1, 0)

    def near(i, c):
        attend(i, s * half, out_own, False)
        return c

    near(0, 0)
    near(1, 0)
    own_cp = pltpu.make_async_copy(
        out_own, out_hbm.at[0, :, pl.ds(pl.multiple_of(s * width, width), width)], loc_sem.at[2])
    own_cp.start()

    def sends_z(k, c):
        l1_copy(k, z).wait_send()
        m1_copy(k, z).wait_send()
        return c

    def sends_p(k, c):
        l2_copy(k, p).wait_send()
        m2_copy(k, p).wait_send()
        return c

    lax.fori_loop(1, NZ, sends_z, 0)
    lax.fori_loop(1, 2 * ND, sends_p, 0)

    def o_wait(i, c):
        o_copy(i, 1 - s).wait_recv()
        o_copy(i, s).wait_send()
        return c

    sq_cp.wait_send()
    lax.fori_loop(0, chunks, o_wait, 0)
    own_cp.wait()


def per_device(latents, timestep, boundary, order, lengths, embed_weight, mod_table, qkv_weight, qk_gain):
    patch, feats = embed_weight.shape[1:]
    width = qkv_weight.shape[3]
    chunks = width // CW
    steps = mod_table.shape[1]
    table = jnp.transpose(mod_table[0], (1, 2, 0)).reshape(-1, steps)
    weights = jnp.transpose(qkv_weight[0], (1, 0, 2))
    tokens, half = 256, 128
    smem = pl.BlockSpec(memory_space=pltpu.SMEM)
    vmem = pl.BlockSpec(memory_space=pltpu.VMEM)
    anywhere = pl.BlockSpec(memory_space=pl.ANY)
    dma = pltpu.SemaphoreType.DMA
    return pl.pallas_call(
        kernel,
        out_shape=jax.ShapeDtypeStruct((1, half, 2 * width), BF16),
        in_specs=[smem] * 4 + [vmem] * 2 + [anywhere] * 3,
        out_specs=anywhere,
        scratch_shapes=[
            pltpu.VMEM((patch, feats), BF16),
            pltpu.VMEM(table.shape, F32),
            pltpu.VMEM((3 * chunks, feats, CW), BF16),
            pltpu.VMEM((NZ, patch, half), BF16),
            pltpu.VMEM((ND, patch, half), BF16),
            pltpu.VMEM((2 * ND, patch, half), BF16),
            pltpu.VMEM((NZ, ND, 128), F32),
            pltpu.VMEM((NZ, ND, 128), F32),
            pltpu.VMEM((ND, NZ, 128), F32),
            pltpu.VMEM((2 * ND, NZ, 128), F32),
            pltpu.VMEM((2, feats), F32),
            pltpu.VMEM((tokens, patch), BF16),
            pltpu.VMEM((tokens, feats), BF16),
            pltpu.VMEM((2 * chunks, tokens, CW), F32),
            pltpu.VMEM((chunks, tokens, CW), BF16),
            pltpu.VMEM((chunks, tokens, CW), BF16),
            pltpu.VMEM((2, 8, tokens), F32),
            pltpu.VMEM((2, 8, tokens), F32),
            pltpu.VMEM((2, tokens, 128), F32),
            pltpu.VMEM((half, width), BF16),
            pltpu.VMEM((half, width), BF16),
            dma((3,)),
            dma((3 * chunks,)),
            dma((NZ,)), dma((NZ,)), dma((NZ,)), dma((NZ,)),
            dma((2 * ND,)), dma((2 * ND,)), dma((2 * ND,)), dma((2 * ND,)),
            dma((2,)),
            dma((chunks,)), dma((chunks,)),
        ],
        compiler_params=pltpu.CompilerParams(
            collective_id=0, has_side_effects=True, vmem_limit_bytes=57 * 1024 * 1024),
        cost_estimate=pl.CostEstimate(flops=13 * 10**9, bytes_accessed=49 * 10**6, transcendentals=800000),
    )(order, timestep, boundary, lengths, latents, qk_gain, embed_weight, table, weights)


def solution(mesh):
    in_specs = (
        P("group", None, "seq"),
        P(),
        P(),
        P(),
        P(),
        P("expert", None, None),
        P("expert", None, None, ("group", "seq")),
        P("expert", None, None, "seq"),
        P("expert", None, "seq"),
    )
    out_specs = P(("expert", "group"), "seq", None)
    return jax.shard_map(
        per_device, mesh=mesh, in_specs=in_specs, out_specs=out_specs, check_vma=False
    )
```

```python
import jax
import jax.numpy as jnp
from jax import lax
from jax.experimental import pallas as pl
from jax.experimental.pallas import tpu as pltpu
from jax.sharding import PartitionSpec as P

HD = 128
EPS = 1e-06
MESH = pl.DeviceIdType.MESH
F32 = jnp.float32
BF16 = jnp.bfloat16
NZ = 8
ND = 8
CW = 256
HI = lax.Precision.HIGHEST
UNROLL = 6
NORM = 20
PAIRS = 3


def kernel(
    order_s, time_s, bound_s, len_s, lat_ref, gain_ref, emb_hbm, tab_hbm, w_hbm,
    out_hbm,
    emb_v, tab_v, wbuf,
    lat_all, lat_send, lat_recv, mod_src, mod_all, mod_send, mod_recv, mod_row,
    xt, normed, proj, vbuf, kbuf, sq_send, sq_recv, inv_qk, out_far, out_own,
    loc_sem, w_sem, l1_send, l1_recv, m1_send, m1_recv, l2_send, l2_recv, m2_send, m2_recv,
    sq_sem, o_send, o_recv,
):
    g = lax.axis_index("group")
    s = lax.axis_index("seq")
    e = lax.axis_index("expert")
    z = g // ND
    d = g % ND
    p = d * 2 + s
    reqs = NZ * ND
    tokens = 256
    half = 128
    feats = emb_v.shape[1]
    chunks = w_hbm.shape[2] // CW
    width = w_hbm.shape[2]

    emb_cp = pltpu.make_async_copy(emb_hbm.at[0], emb_v, loc_sem.at[0])
    tab_cp = pltpu.make_async_copy(tab_hbm, tab_v, loc_sem.at[1])
    tab_cp.start()
    emb_cp.start()

    def w_copy(i):
        return pltpu.make_async_copy(
            w_hbm.at[i // chunks, :, pl.ds(pl.multiple_of((i % chunks) * CW, CW), CW)],
            wbuf.at[i], w_sem.at[i],
        )

    def w_start(i, c):
        w_copy(i).start()
        return c

    lax.fori_loop(0, 3 * chunks, w_start, 0)

    barrier = pltpu.get_barrier_semaphore()

    def greet_z(k, c):
        pl.semaphore_signal(barrier, inc=1, device_id={"group": ((z + k) % NZ) * ND + d}, device_id_type=MESH)
        return c

    def greet_p(k, c):
        q = (p + k) % (2 * ND)
        pl.semaphore_signal(barrier, inc=1, device_id={"group": z * ND + q // 2, "seq": q % 2}, device_id_type=MESH)
        return c

    lax.fori_loop(1, NZ, greet_z, 0)
    lax.fori_loop(1, 2 * ND, greet_p, 0)
    pl.semaphore_wait(barrier, NZ - 1 + 2 * ND - 1)

    def l1_copy(k, slot):
        return pltpu.make_async_remote_copy(
            src_ref=lat_ref.at[0], dst_ref=lat_all.at[slot], send_sem=l1_send.at[k], recv_sem=l1_recv.at[slot],
            device_id={"group": ((z + k) % NZ) * ND + d}, device_id_type=MESH)

    def l1_start(k, c):
        l1_copy(k, z).start()
        return c

    lax.fori_loop(1, NZ, l1_start, 0, unroll=True)
    lat_all[z] = lat_ref[0]

    rows = lax.broadcasted_iota(jnp.int32, (reqs, 128), 0)

    def pick(r, c):
        col, stamp, live = c
        where = order_s[r]
        col = jnp.where(rows == where, time_s[r], col)
        mine = where == g
        return col, jnp.where(mine, time_s[r], stamp), jnp.where(mine, len_s[r], live)

    col, stamp, live = lax.fori_loop(
        0, reqs, pick, (jnp.zeros((reqs, 128), jnp.int32), jnp.int32(0), jnp.int32(0)), unroll=8)
    expert_of = jnp.where(stamp >= bound_s[0], 0, 1)
    shown = jnp.where(expert_of == e, live, 0)

    steps = tab_v.shape[1]
    tab_cp.wait()
    hit = jnp.where(lax.broadcasted_iota(jnp.int32, (reqs, steps), 1) == col[:, :1], 1.0, 0.0).astype(BF16)

    def picked_of(part):
        return lax.dot_general(hit, part, (((1,), (1,)), ((), ())), preferred_element_type=F32)

    part_a = tab_v[...].astype(BF16)
    rest = tab_v[...] - part_a.astype(F32)
    part_b = rest.astype(BF16)
    part_c = (rest - part_b.astype(F32)).astype(BF16)
    picked = picked_of(part_a) + (picked_of(part_b) + picked_of(part_c))
    mod_src[...] = jnp.zeros_like(mod_src)
    for a in range(NZ):
        mod_src[a, :, : tab_v.shape[0]] = picked[a * ND : (a + 1) * ND]

    def m1_copy(k, slot):
        z2 = (z + k) % NZ
        return pltpu.make_async_remote_copy(
            src_ref=mod_src.at[z2], dst_ref=mod_all.at[slot], send_sem=m1_send.at[k], recv_sem=m1_recv.at[slot],
            device_id={"group": z2 * ND + d}, device_id_type=MESH)

    def m1_start(k, c):
        m1_copy(k, z).start()
        return c

    lax.fori_loop(1, NZ, m1_start, 0, unroll=True)
    mod_all[z] = mod_src[z]

    def l1_wait(k, c):
        l1_copy(k, (z + k) % NZ).wait_recv()
        return c

    lax.fori_loop(1, NZ, l1_wait, 0)
    for b in range(ND):
        chosen = jnp.zeros(lat_all.shape[1:], BF16)
        for a in range(NZ):
            chosen = jnp.where(order_s[a * ND + d] == z * ND + b, lat_all[a], chosen)
        lat_send[b] = chosen

    def l2_copy(k, slot):
        q = (p + k) % (2 * ND)
        return pltpu.make_async_remote_copy(
            src_ref=lat_send.at[q // 2], dst_ref=lat_recv.at[slot], send_sem=l2_send.at[k], recv_sem=l2_recv.at[slot],
            device_id={"group": z * ND + q // 2, "seq": q % 2}, device_id_type=MESH)

    def l2_start(k, c):
        l2_copy(k, p).start()
        return c

    lax.fori_loop(1, 2 * ND, l2_start, 0, unroll=5)
    lat_recv[p] = lat_send[d]

    def m1_wait(k, c):
        m1_copy(k, (z + k) % NZ).wait_recv()
        return c

    lax.fori_loop(1, NZ, m1_wait, 0)
    for b in range(ND):
        for a in range(NZ):
            mod_send[b, a : a + 1] = mod_all[a, b : b + 1]

    def m2_copy(k, slot):
        q = (p + k) % (2 * ND)
        return pltpu.make_async_remote_copy(
            src_ref=mod_send.at[q // 2], dst_ref=mod_recv.at[slot], send_sem=m2_send.at[k], recv_sem=m2_recv.at[slot],
            device_id={"group": z * ND + q // 2, "seq": q % 2}, device_id_type=MESH)

    def m2_start(k, c):
        m2_copy(k, p).start()
        return c

    lax.fori_loop(1, 2 * ND, m2_start, 0, unroll=5)
    mod_recv[p] = mod_send[d]

    emb_cp.wait()
    wbar = jnp.sum(emb_v[...].astype(F32), axis=1, keepdims=True) * (1.0 / feats)
    et = 256
    tiles = feats // et

    def gram_step(i, gram):
        centred = emb_v[:, pl.ds(pl.multiple_of(i * et, et), et)].astype(F32) - wbar
        return gram + lax.dot_general(
            centred, centred, (((1,), (1,)), ((), ())), precision=HI, preferred_element_type=F32)

    patch = emb_v.shape[0]
    gram = lax.fori_loop(0, tiles, gram_step, jnp.zeros((patch, patch), F32), unroll=4) * (1.0 / feats)
    wbar = jnp.broadcast_to(wbar, (patch, 128))

    def l2_wait(k, c):
        l2_copy(k, (p + k) % (2 * ND)).wait_recv()
        return c

    lax.fori_loop(1, 2 * ND, l2_wait, 0)
    for t in range(2):
        x = lat_recv[t].astype(F32)
        for b in range(1, ND):
            x = x + lat_recv[2 * b + t].astype(F32)
        xt[t * half : (t + 1) * half] = jnp.transpose(x).astype(BF16)

    xf = xt[...].astype(F32)
    mean = jnp.dot(xf, wbar, precision=HI, preferred_element_type=F32)
    var = jnp.sum(jnp.dot(xf, gram, precision=HI, preferred_element_type=F32) * xf, axis=1, keepdims=True)
    rstd = jnp.broadcast_to(1.0 / jnp.sqrt(jnp.maximum(var, 0.0) + EPS), (tokens, 128))

    def m2_wait(k, c):
        m2_copy(k, (p + k) % (2 * ND)).wait_recv()
        return c

    lax.fori_loop(1, 2 * ND, m2_wait, 0)
    own = tab_v.shape[0] // 2
    lane = lax.broadcasted_iota(jnp.int32, (NZ, 128), 1)
    span = 2 * ND * own // 128
    for c in range(2):
        pieces = [jnp.zeros((NZ, 128), F32) for _ in range(span)]
        for q in range(2 * ND):
            start = q * own
            off = start % 128
            turned = pltpu.roll(mod_recv[q], (off - c * own) % 128, 1)
            a = start // 128
            pieces[a] = jnp.where((lane >= off) & (lane < off + own), turned, pieces[a])
            if off + own > 128:
                pieces[a + 1] = jnp.where(lane < off + own - 128, turned, pieces[a + 1])
        for a in range(span):
            for b in range(NZ):
                n = (b * span + a) * 128
                mod_row[c : c + 1, n : n + 128] = pieces[a][b : b + 1] + float(c)

    for t in range(2):
        rows_t = slice(t * half, (t + 1) * half)

        def modulate(i, c, rows_t=rows_t):
            made = jnp.dot(xt[rows_t], emb_v[:, pl.ds(pl.multiple_of(i * et, et), et)], preferred_element_type=F32)
            for h in range(et // 128):
                cols = pl.ds(pl.multiple_of(i * et + h * 128, 128), 128)
                v = (made[:, h * 128 : (h + 1) * 128] - mean[rows_t]) * rstd[rows_t]
                normed[rows_t, cols] = (v * mod_row[1:2, cols] + mod_row[0:1, cols]).astype(BF16)
            return c

        lax.fori_loop(0, tiles, modulate, 0, unroll=NORM)

    def arrive(base):
        def body(i, c):
            w_copy(base + i).wait()
            return c
        lax.fori_loop(0, chunks, body, 0)

    def project(i):
        return jnp.dot(normed[...], wbuf[i], preferred_element_type=F32)

    def squares(base):
        def body(i, ss):
            made = project(base + i)
            proj[base + i] = made
            made = made * made
            return ss + (made[:, :128] + made[:, 128:])
        return lax.fori_loop(0, chunks, body, jnp.zeros((tokens, 128), F32), unroll=UNROLL)

    ones = jnp.ones((8, 128), F32)

    def as_rows(ss):
        return lax.dot_general(ones, ss, (((1,), (1,)), ((), ())), precision=HI, preferred_element_type=F32)

    arrive(0)
    q_ss = squares(0)
    arrive(chunks)
    k_ss = squares(chunks)
    sq_send[0] = as_rows(q_ss)
    sq_send[1] = as_rows(k_ss)
    sq_cp = pltpu.make_async_remote_copy(
        src_ref=sq_send, dst_ref=sq_recv, send_sem=sq_sem.at[0], recv_sem=sq_sem.at[1],
        device_id={"seq": 1 - s}, device_id_type=MESH)
    sq_cp.start()

    def values(i, c):
        vbuf[i] = project(2 * chunks + i).astype(BF16)
        return c

    first = chunks // 2
    arrive(2 * chunks)
    lax.fori_loop(0, first, values, 0, unroll=UNROLL)
    sq_cp.wait_recv()
    for c in range(2):
        total = sq_send[c] + sq_recv[c]
        inv = 1.0 / jnp.sqrt(total * (1.0 / (2 * width)) + EPS)
        inv = jnp.broadcast_to(inv[0:1], (128, tokens))
        inv_qk[c] = jnp.transpose(inv)

    keypos = lax.broadcasted_iota(jnp.int32, (half, tokens), 1)
    rowpos = lax.broadcasted_iota(jnp.int32, (half, HD), 0)

    def o_copy(i, side):
        cols = pl.ds(pl.multiple_of(i * CW, CW), CW)
        there = pl.ds(pl.multiple_of(side * width + i * CW, CW), CW)
        return pltpu.make_async_remote_copy(
            src_ref=out_far.at[:, cols], dst_ref=out_hbm.at[0, :, there], send_sem=o_send.at[i], recv_sem=o_recv.at[i],
            device_id={"seq": 1 - s}, device_id_type=MESH)

    def attend(i, r0, out_ref, first):
        at = pl.ds(pl.multiple_of(r0, half), half)
        work = []
        for u in range(PAIRS):
            n = i * PAIRS + u
            for j in range(CW // HD):
                hc = slice(j * HD, (j + 1) * HD)
                cols = pl.ds(pl.multiple_of(n * CW + j * HD, HD), HD)
                if first:
                    kbuf[n, :, hc] = (proj[chunks + n, :, hc] * inv_qk[1] * gain_ref[0, 1:2, cols]).astype(BF16)
                qn = (proj[n, at, hc] * inv_qk[0, at, :] * gain_ref[0, 0:1, cols]).astype(BF16)
                work.append((n, hc, cols, qn))
        scores = [lax.dot_general(qn, kbuf[n, :, hc], (((1,), (1,)), ((), ())), preferred_element_type=F32)
                  for n, hc, _, qn in work]
        parts = []
        for sc in scores:
            sc = jnp.where(keypos < live, sc * HD ** (-0.5), -jnp.inf)
            ex = jnp.exp(sc - jnp.max(sc, axis=1, keepdims=True))
            parts.append((ex * (1.0 / jnp.sum(ex, axis=1, keepdims=True))).astype(BF16))
        for k, ((n, hc, cols, _), pr) in enumerate(zip(work, parts)):
            mixed = jnp.dot(pr, vbuf[n, :, hc], preferred_element_type=F32)
            out_ref[:, cols] = jnp.where(rowpos + r0 < shown, mixed, 0.0).astype(BF16)
            if first and k % 2 == 1:
                o_copy(n, s).start()

    def far(i, c):
        attend(i, (1 - s) * half, out_far, True)
        return c

    far(0, 0)
    lax.fori_loop(first, chunks, values, 0, unroll=UNROLL)
    far(1, 0)

    def near(i, c):
        attend(i, s * half, out_own, False)
        return c

    near(0, 0)
    near(1, 0)
    own_cp = pltpu.make_async_copy(
        out_own, out_hbm.at[0, :, pl.ds(pl.multiple_of(s * width, width), width)], loc_sem.at[2])
    own_cp.start()

    def sends_z(k, c):
        l1_copy(k, z).wait_send()
        m1_copy(k, z).wait_send()
        return c

    def sends_p(k, c):
        l2_copy(k, p).wait_send()
        m2_copy(k, p).wait_send()
        return c

    lax.fori_loop(1, NZ, sends_z, 0)
    lax.fori_loop(1, 2 * ND, sends_p, 0)

    def o_wait(i, c):
        o_copy(i, 1 - s).wait_recv()
        o_copy(i, s).wait_send()
        return c

    sq_cp.wait_send()
    lax.fori_loop(0, chunks, o_wait, 0)
    own_cp.wait()


def per_device(latents, timestep, boundary, order, lengths, embed_weight, mod_table, qkv_weight, qk_gain):
    patch, feats = embed_weight.shape[1:]
    width = qkv_weight.shape[3]
    chunks = width // CW
    steps = mod_table.shape[1]
    table = jnp.transpose(mod_table[0], (1, 2, 0)).reshape(-1, steps)
    weights = jnp.transpose(qkv_weight[0], (1, 0, 2))
    tokens, half = 256, 128
    smem = pl.BlockSpec(memory_space=pltpu.SMEM)
    vmem = pl.BlockSpec(memory_space=pltpu.VMEM)
    anywhere = pl.BlockSpec(memory_space=pl.ANY)
    dma = pltpu.SemaphoreType.DMA
    return pl.pallas_call(
        kernel,
        out_shape=jax.ShapeDtypeStruct((1, half, 2 * width), BF16),
        in_specs=[smem] * 4 + [vmem] * 2 + [anywhere] * 3,
        out_specs=anywhere,
        scratch_shapes=[
            pltpu.VMEM((patch, feats), BF16),
            pltpu.VMEM(table.shape, F32),
            pltpu.VMEM((3 * chunks, feats, CW), BF16),
            pltpu.VMEM((NZ, patch, half), BF16),
            pltpu.VMEM((ND, patch, half), BF16),
            pltpu.VMEM((2 * ND, patch, half), BF16),
            pltpu.VMEM((NZ, ND, 128), F32),
            pltpu.VMEM((NZ, ND, 128), F32),
            pltpu.VMEM((ND, NZ, 128), F32),
            pltpu.VMEM((2 * ND, NZ, 128), F32),
            pltpu.VMEM((2, feats), F32),
            pltpu.VMEM((tokens, patch), BF16),
            pltpu.VMEM((tokens, feats), BF16),
            pltpu.VMEM((2 * chunks, tokens, CW), F32),
            pltpu.VMEM((chunks, tokens, CW), BF16),
            pltpu.VMEM((chunks, tokens, CW), BF16),
            pltpu.VMEM((2, 8, tokens), F32),
            pltpu.VMEM((2, 8, tokens), F32),
            pltpu.VMEM((2, tokens, 128), F32),
            pltpu.VMEM((half, width), BF16),
            pltpu.VMEM((half, width), BF16),
            dma((3,)),
            dma((3 * chunks,)),
            dma((NZ,)), dma((NZ,)), dma((NZ,)), dma((NZ,)),
            dma((2 * ND,)), dma((2 * ND,)), dma((2 * ND,)), dma((2 * ND,)),
            dma((2,)),
            dma((chunks,)), dma((chunks,)),
        ],
        compiler_params=pltpu.CompilerParams(
            collective_id=0, has_side_effects=True, vmem_limit_bytes=57 * 1024 * 1024),
        cost_estimate=pl.CostEstimate(flops=13 * 10**9, bytes_accessed=49 * 10**6, transcendentals=800000),
    )(order, timestep, boundary, lengths, latents, qk_gain, embed_weight, table, weights)


def solution(mesh):
    in_specs = (
        P("group", None, "seq"),
        P(),
        P(),
        P(),
        P(),
        P("expert", None, None),
        P("expert", None, None, ("group", "seq")),
        P("expert", None, None, "seq"),
        P("expert", None, "seq"),
    )
    out_specs = P(("expert", "group"), "seq", None)
    return jax.shard_map(
        per_device, mesh=mesh, in_specs=in_specs, out_specs=out_specs, check_vma=False
    )
```

```python
import functools

import jax
import jax.numpy as jnp
from jax import lax
from jax.experimental import pallas as pl
from jax.experimental.pallas import tpu as pltpu
from jax.sharding import PartitionSpec as P

HD = 128
EPS = 1e-06
MESH = pl.DeviceIdType.MESH
F32 = jnp.float32
BF16 = jnp.bfloat16
NZ = 8
ND = 8
CW = 256
HI = lax.Precision.HIGHEST
UNROLL = 6
NORM = 20
SLOTS = 14
PAIRS = 3


def kernel(
    order_hbm, time_hbm, bound_s, len_hbm, lat_hbm, gain_hbm, emb_hbm, tab_hbm, w_hbm,
    out_hbm,
    order_s, time_s, len_s, lat_ref, gain_ref, emb_v, tab_v, wbuf,
    lat_all, lat_send, lat_recv, mod_src, mod_all, mod_send, mod_recv, mod_row,
    right_v, xt, normed, proj, vbuf, kbuf, sq_send, sq_recv, inv_qk, out_far, out_own,
    loc_sem, w_sem, l1_send, l1_recv, m1_send, m1_recv, l2_send, l2_recv, m2_send, m2_recv,
    sq_sem, o_send, o_recv,
):
    g = lax.axis_index("group")
    s = lax.axis_index("seq")
    e = lax.axis_index("expert")
    z = g // ND
    d = g % ND
    p = d * 2 + s
    reqs = NZ * ND
    tokens = 256
    half = 128
    feats = emb_v.shape[1]
    chunks = w_hbm.shape[2] // CW
    width = w_hbm.shape[2]

    emb_cp = pltpu.make_async_copy(emb_hbm.at[0], emb_v, loc_sem.at[0])
    tab_cp = pltpu.make_async_copy(tab_hbm, tab_v, loc_sem.at[1])
    small = [
        pltpu.make_async_copy(src, dst, loc_sem.at[3 + k])
        for k, (src, dst) in enumerate([
            (lat_hbm, lat_ref), (order_hbm, order_s), (time_hbm, time_s), (len_hbm, len_s), (gain_hbm, gain_ref)])
    ]
    for cp in small[:4]:
        cp.start()
    tab_cp.start()
    emb_cp.start()
    small[4].start()

    def w_copy(i):
        return pltpu.make_async_copy(
            w_hbm.at[i // chunks, :, pl.ds(pl.multiple_of((i % chunks) * CW, CW), CW)],
            wbuf.at[i % SLOTS], w_sem.at[i],
        )

    def w_start(i, c):
        w_copy(i).start()
        return c

    lax.fori_loop(0, SLOTS, w_start, 0)

    barrier = pltpu.get_barrier_semaphore()

    def greet_z(k, c):
        pl.semaphore_signal(barrier, inc=1, device_id={"group": ((z + k) % NZ) * ND + d}, device_id_type=MESH)
        return c

    def greet_p(k, c):
        q = (p + k) % (2 * ND)
        pl.semaphore_signal(barrier, inc=1, device_id={"group": z * ND + q // 2, "seq": q % 2}, device_id_type=MESH)
        return c

    lax.fori_loop(1, NZ, greet_z, 0)
    lax.fori_loop(1, 2 * ND, greet_p, 0)
    pl.semaphore_wait(barrier, NZ - 1 + 2 * ND - 1)

    small[0].wait()

    def l1_copy(k, slot):
        return pltpu.make_async_remote_copy(
            src_ref=lat_ref.at[0], dst_ref=lat_all.at[slot], send_sem=l1_send.at[k], recv_sem=l1_recv.at[slot],
            device_id={"group": ((z + k) % NZ) * ND + d}, device_id_type=MESH)

    def l1_start(k, c):
        l1_copy(k, z).start()
        return c

    lax.fori_loop(1, NZ, l1_start, 0, unroll=True)
    lat_all[z] = lat_ref[0]

    for cp in small[1:4]:
        cp.wait()

    rows = lax.broadcasted_iota(jnp.int32, (reqs, 128), 0)

    def pick(r, c):
        col, stamp, live = c
        where = order_s[r]
        col = jnp.where(rows == where, time_s[r], col)
        mine = where == g
        return col, jnp.where(mine, time_s[r], stamp), jnp.where(mine, len_s[r], live)

    col, stamp, live = lax.fori_loop(
        0, reqs, pick, (jnp.zeros((reqs, 128), jnp.int32), jnp.int32(0), jnp.int32(0)), unroll=8)
    expert_of = jnp.where(stamp >= bound_s[0], 0, 1)
    shown = jnp.where(expert_of == e, live, 0)

    steps = tab_v.shape[1]
    tab_cp.wait()
    hit = jnp.where(lax.broadcasted_iota(jnp.int32, (reqs, steps), 1) == col[:, :1], 1.0, 0.0).astype(BF16)

    def picked_of(part):
        return lax.dot_general(hit, part, (((1,), (1,)), ((), ())), preferred_element_type=F32)

    part_a = tab_v[...].astype(BF16)
    rest = tab_v[...] - part_a.astype(F32)
    part_b = rest.astype(BF16)
    part_c = (rest - part_b.astype(F32)).astype(BF16)
    picked = picked_of(part_a) + (picked_of(part_b) + picked_of(part_c))
    mod_src[...] = jnp.zeros_like(mod_src)
    for a in range(NZ):
        mod_src[a, :, : tab_v.shape[0]] = picked[a * ND : (a + 1) * ND]

    def m1_copy(k, slot):
        z2 = (z + k) % NZ
        return pltpu.make_async_remote_copy(
            src_ref=mod_src.at[z2], dst_ref=mod_all.at[slot], send_sem=m1_send.at[k], recv_sem=m1_recv.at[slot],
            device_id={"group": z2 * ND + d}, device_id_type=MESH)

    def m1_start(k, c):
        m1_copy(k, z).start()
        return c

    lax.fori_loop(1, NZ, m1_start, 0, unroll=True)
    mod_all[z] = mod_src[z]

    def l1_wait(k, c):
        l1_copy(k, (z + k) % NZ).wait_recv()
        return c

    lax.fori_loop(1, NZ, l1_wait, 0)
    for b in range(ND):
        chosen = jnp.zeros(lat_all.shape[1:], BF16)
        for a in range(NZ):
            chosen = jnp.where(order_s[a * ND + d] == z * ND + b, lat_all[a], chosen)
        lat_send[b] = chosen

    def l2_copy(k, slot):
        q = (p + k) % (2 * ND)
        return pltpu.make_async_remote_copy(
            src_ref=lat_send.at[q // 2], dst_ref=lat_recv.at[slot], send_sem=l2_send.at[k], recv_sem=l2_recv.at[slot],
            device_id={"group": z * ND + q // 2, "seq": q % 2}, device_id_type=MESH)

    def l2_start(k, c):
        l2_copy(k, p).start()
        return c

    lax.fori_loop(1, 2 * ND, l2_start, 0, unroll=5)
    lat_recv[p] = lat_send[d]

    def m1_wait(k, c):
        m1_copy(k, (z + k) % NZ).wait_recv()
        return c

    lax.fori_loop(1, NZ, m1_wait, 0)
    for b in range(ND):
        for a in range(NZ):
            mod_send[b, a : a + 1] = mod_all[a, b : b + 1]

    def m2_copy(k, slot):
        q = (p + k) % (2 * ND)
        return pltpu.make_async_remote_copy(
            src_ref=mod_send.at[q // 2], dst_ref=mod_recv.at[slot], send_sem=m2_send.at[k], recv_sem=m2_recv.at[slot],
            device_id={"group": z * ND + q // 2, "seq": q % 2}, device_id_type=MESH)

    def m2_start(k, c):
        m2_copy(k, p).start()
        return c

    lax.fori_loop(1, 2 * ND, m2_start, 0, unroll=5)
    mod_recv[p] = mod_send[d]

    emb_cp.wait()
    wbar = jnp.sum(emb_v[...].astype(F32), axis=1, keepdims=True) * (1.0 / feats)
    et = 256
    tiles = feats // et

    def gram_step(i, gram):
        centred = emb_v[:, pl.ds(pl.multiple_of(i * et, et), et)].astype(F32) - wbar
        return gram + lax.dot_general(
            centred, centred, (((1,), (1,)), ((), ())), precision=HI, preferred_element_type=F32)

    patch = emb_v.shape[0]
    gram = lax.fori_loop(0, tiles, gram_step, jnp.zeros((patch, patch), F32), unroll=4) * (1.0 / feats)
    right = jnp.concatenate([jnp.broadcast_to(wbar, (patch, 128)), gram, jnp.zeros((patch, 128 - patch), F32)], axis=1)
    for k in range(3):
        part = right.astype(BF16)
        right_v[k] = part
        right = right - part.astype(F32)

    def l2_wait(k, c):
        l2_copy(k, (p + k) % (2 * ND)).wait_recv()
        return c

    lax.fori_loop(1, 2 * ND, l2_wait, 0)
    for t in range(2):
        x = lat_recv[t].astype(F32)
        for b in range(1, ND):
            x = x + lat_recv[2 * b + t].astype(F32)
        xt[t * half : (t + 1) * half] = jnp.transpose(x).astype(BF16)

    xb = xt[...]
    both = [jnp.dot(xb, right_v[k], preferred_element_type=F32) for k in range(3)]
    both = both[0] + (both[1] + both[2])
    mean = both[:, :128]
    var = jnp.sum(both[:, 128 : 128 + patch] * xb.astype(F32), axis=1, keepdims=True)
    rstd = jnp.broadcast_to(1.0 / jnp.sqrt(jnp.maximum(var, 0.0) + EPS), (tokens, 128))

    def m2_wait(k, c):
        m2_copy(k, (p + k) % (2 * ND)).wait_recv()
        return c

    lax.fori_loop(1, 2 * ND, m2_wait, 0)
    own = tab_v.shape[0] // 2
    lane = lax.broadcasted_iota(jnp.int32, (NZ, 128), 1)
    span = 2 * ND * own // 128
    for c in range(2):
        pieces = [jnp.zeros((NZ, 128), F32) for _ in range(span)]
        for q in range(2 * ND):
            start = q * own
            off = start % 128
            turned = pltpu.roll(mod_recv[q], (off - c * own) % 128, 1)
            a = start // 128
            pieces[a] = jnp.where((lane >= off) & (lane < off + own), turned, pieces[a])
            if off + own > 128:
                pieces[a + 1] = jnp.where(lane < off + own - 128, turned, pieces[a + 1])
        for a in range(span):
            for b in range(NZ):
                n = (b * span + a) * 128
                mod_row[c : c + 1, n : n + 128] = pieces[a][b : b + 1] + float(c)

    def arrive(i, c):
        w_copy(i).wait()
        return c

    lax.fori_loop(0, chunks, arrive, 0)

    def modulate(i, c):
        tile = pl.ds(pl.multiple_of(i * et, et), et)
        for t in range(2):
            rows_t = slice(t * half, (t + 1) * half)
            made = jnp.dot(xt[rows_t], emb_v[:, tile], preferred_element_type=F32)
            for h in range(et // 128):
                cols = pl.ds(pl.multiple_of(i * et + h * 128, 128), 128)
                v = (made[:, h * 128 : (h + 1) * 128] - mean[rows_t]) * rstd[rows_t]
                normed[rows_t, cols] = (v * mod_row[1:2, cols] + mod_row[0:1, cols]).astype(BF16)
        return c

    lax.fori_loop(0, tiles, modulate, 0, unroll=NORM)

    def project(i):
        return jnp.dot(normed[...], wbuf[i % SLOTS], preferred_element_type=F32)

    def squares(base):
        def body(i, ss):
            made = project(base + i)
            proj[base + i] = made
            made = made * made
            return ss + (made[:, :128] + made[:, 128:])
        return lax.fori_loop(0, chunks, body, jnp.zeros((tokens, 128), F32), unroll=UNROLL)

    ones = jnp.ones((8, 128), F32)

    def as_rows(ss):
        return lax.dot_general(ones, ss, (((1,), (1,)), ((), ())), precision=HI, preferred_element_type=F32)

    q_ss = squares(0)
    lax.fori_loop(SLOTS, 3 * chunks, w_start, 0)
    lax.fori_loop(chunks, 2 * chunks, arrive, 0)
    k_ss = squares(chunks)
    sq_send[0] = as_rows(q_ss)
    sq_send[1] = as_rows(k_ss)
    sq_cp = pltpu.make_async_remote_copy(
        src_ref=sq_send, dst_ref=sq_recv, send_sem=sq_sem.at[0], recv_sem=sq_sem.at[1],
        device_id={"seq": 1 - s}, device_id_type=MESH)
    sq_cp.start()

    def values(i, c):
        vbuf[i] = project(2 * chunks + i).astype(BF16)
        return c

    first = chunks // 2
    lax.fori_loop(2 * chunks, 3 * chunks, arrive, 0)
    small[4].wait()
    lax.fori_loop(0, first, values, 0, unroll=first)
    sq_cp.wait_recv()
    for c in range(2):
        total = sq_send[c] + sq_recv[c]
        inv = 1.0 / jnp.sqrt(total * (1.0 / (2 * width)) + EPS)
        inv = jnp.broadcast_to(inv[0:1], (128, tokens))
        inv_qk[c] = jnp.transpose(inv)

    keypos = lax.broadcasted_iota(jnp.int32, (half, tokens), 1)
    rowpos = lax.broadcasted_iota(jnp.int32, (half, HD), 0)

    def o_copy(i, side):
        cols = pl.ds(pl.multiple_of(i * CW, CW), CW)
        there = pl.ds(pl.multiple_of(side * width + i * CW, CW), CW)
        return pltpu.make_async_remote_copy(
            src_ref=out_far.at[:, cols], dst_ref=out_hbm.at[0, :, there], send_sem=o_send.at[i], recv_sem=o_recv.at[i],
            device_id={"seq": 1 - s}, device_id_type=MESH)

    def attend(i, r0, out_ref, first):
        at = pl.ds(pl.multiple_of(r0, half), half)
        work = []
        for u in range(PAIRS):
            n = i * PAIRS + u
            for j in range(CW // HD):
                hc = slice(j * HD, (j + 1) * HD)
                cols = pl.ds(pl.multiple_of(n * CW + j * HD, HD), HD)
                if first:
                    kbuf[n, :, hc] = (proj[chunks + n, :, hc] * inv_qk[1] * gain_ref[0, 1:2, cols]).astype(BF16)
                qn = (proj[n, at, hc] * inv_qk[0, at, :] * gain_ref[0, 0:1, cols]).astype(BF16)
                work.append((n, hc, cols, qn))
        scores = [lax.dot_general(qn, kbuf[n, :, hc], (((1,), (1,)), ((), ())), preferred_element_type=F32)
                  for n, hc, _, qn in work]
        parts = []
        for sc in scores:
            sc = jnp.where(keypos < live, sc * HD ** (-0.5), -jnp.inf)
            ex = jnp.exp(sc - jnp.max(sc, axis=1, keepdims=True))
            parts.append((ex * (1.0 / jnp.sum(ex, axis=1, keepdims=True))).astype(BF16))
        for k, ((n, hc, cols, _), pr) in enumerate(zip(work, parts)):
            mixed = jnp.dot(pr, vbuf[n, :, hc], preferred_element_type=F32)
            out_ref[:, cols] = jnp.where(rowpos + r0 < shown, mixed, 0.0).astype(BF16)
            if first and k % 2 == 1:
                o_copy(n, s).start()

    def far(i, c):
        attend(i, (1 - s) * half, out_far, True)
        return c

    far(0, 0)
    lax.fori_loop(first, chunks, values, 0, unroll=first)
    far(1, 0)

    def near(i, c):
        attend(i, s * half, out_own, False)
        return c

    near(0, 0)
    near(1, 0)
    own_cp = pltpu.make_async_copy(
        out_own, out_hbm.at[0, :, pl.ds(pl.multiple_of(s * width, width), width)], loc_sem.at[2])
    own_cp.start()

    def sends_z(k, c):
        l1_copy(k, z).wait_send()
        m1_copy(k, z).wait_send()
        return c

    def sends_p(k, c):
        l2_copy(k, p).wait_send()
        m2_copy(k, p).wait_send()
        return c

    lax.fori_loop(1, NZ, sends_z, 0)
    lax.fori_loop(1, 2 * ND, sends_p, 0)

    def o_wait(i, c):
        o_copy(i, 1 - s).wait_recv()
        o_copy(i, s).wait_send()
        return c

    sq_cp.wait_send()
    lax.fori_loop(0, chunks, o_wait, 0)
    own_cp.wait()


def per_device(latents, timestep, boundary, order, lengths, embed_weight, mod_table, qkv_weight, qk_gain):
    patch, feats = embed_weight.shape[1:]
    width = qkv_weight.shape[3]
    chunks = width // CW
    steps = mod_table.shape[1]
    table = jnp.transpose(mod_table[0], (1, 2, 0)).reshape(-1, steps)
    weights = jnp.transpose(qkv_weight[0], (1, 0, 2))
    tokens, half = 256, 128
    keep = functools.partial(pltpu.with_memory_space_constraint, memory_space=pltpu.HBM)
    smem = pl.BlockSpec(memory_space=pltpu.SMEM)
    hbm = pl.BlockSpec(memory_space=pltpu.HBM)
    anywhere = pl.BlockSpec(memory_space=pl.ANY)
    dma = pltpu.SemaphoreType.DMA
    return pl.pallas_call(
        kernel,
        out_shape=jax.ShapeDtypeStruct((1, half, 2 * width), BF16),
        in_specs=[hbm] * 2 + [smem] + [hbm] * 6,
        out_specs=anywhere,
        scratch_shapes=[
            pltpu.SMEM(order.shape, jnp.int32),
            pltpu.SMEM(timestep.shape, jnp.int32),
            pltpu.SMEM(lengths.shape, jnp.int32),
            pltpu.VMEM(latents.shape, BF16),
            pltpu.VMEM(qk_gain.shape, F32),
            pltpu.VMEM((patch, feats), BF16),
            pltpu.VMEM(table.shape, F32),
            pltpu.VMEM((SLOTS, feats, CW), BF16),
            pltpu.VMEM((NZ, patch, half), BF16),
            pltpu.VMEM((ND, patch, half), BF16),
            pltpu.VMEM((2 * ND, patch, half), BF16),
            pltpu.VMEM((NZ, ND, 128), F32),
            pltpu.VMEM((NZ, ND, 128), F32),
            pltpu.VMEM((ND, NZ, 128), F32),
            pltpu.VMEM((2 * ND, NZ, 128), F32),
            pltpu.VMEM((2, feats), F32),
            pltpu.VMEM((3, patch, 256), BF16),
            pltpu.VMEM((tokens, patch), BF16),
            pltpu.VMEM((tokens, feats), BF16),
            pltpu.VMEM((2 * chunks, tokens, CW), F32),
            pltpu.VMEM((chunks, tokens, CW), BF16),
            pltpu.VMEM((chunks, tokens, CW), BF16),
            pltpu.VMEM((2, 8, tokens), F32),
            pltpu.VMEM((2, 8, tokens), F32),
            pltpu.VMEM((2, tokens, 128), F32),
            pltpu.VMEM((half, width), BF16),
            pltpu.VMEM((half, width), BF16),
            dma((8,)),
            dma((3 * chunks,)),
            dma((NZ,)), dma((NZ,)), dma((NZ,)), dma((NZ,)),
            dma((2 * ND,)), dma((2 * ND,)), dma((2 * ND,)), dma((2 * ND,)),
            dma((2,)),
            dma((chunks,)), dma((chunks,)),
        ],
        compiler_params=pltpu.CompilerParams(
            collective_id=0, has_side_effects=True, vmem_limit_bytes=48 * 1024 * 1024),
        cost_estimate=pl.CostEstimate(flops=13 * 10**9, bytes_accessed=49 * 10**6, transcendentals=800000),
    )(keep(order), keep(timestep), boundary, keep(lengths), keep(latents), keep(qk_gain), keep(embed_weight),
      keep(table), keep(weights))


def solution(mesh):
    in_specs = (
        P("group", None, "seq"),
        P(),
        P(),
        P(),
        P(),
        P("expert", None, None),
        P("expert", None, None, ("group", "seq")),
        P("expert", None, None, "seq"),
        P("expert", None, "seq"),
    )
    out_specs = P(("expert", "group"), "seq", None)
    return jax.shard_map(
        per_device, mesh=mesh, in_specs=in_specs, out_specs=out_specs, check_vma=False
    )
```

```python
import functools

import jax
import jax.numpy as jnp
from jax import lax
from jax.experimental import pallas as pl
from jax.experimental.pallas import tpu as pltpu
from jax.sharding import PartitionSpec as P

HD = 128
EPS = 1e-06
MESH = pl.DeviceIdType.MESH
F32 = jnp.float32
BF16 = jnp.bfloat16
NZ = 8
ND = 8
CW = 256
HI = lax.Precision.HIGHEST
UNROLL = 6
NORM = 20
SLOTS = 14
PAIRS = 3


def kernel(
    order_hbm, time_hbm, bound_s, len_hbm, lat_hbm, gain_hbm, emb_hbm, tab_hbm, w_hbm,
    out_hbm,
    order_s, time_s, len_s, lat_ref, gain_ref, emb_v, tab_v, wbuf,
    lat_all, lat_send, lat_recv, mod_src, mod_all, mod_send, mod_recv, mod_row,
    right_v, xt, normed, proj, vbuf, kbuf, sq_send, sq_recv, inv_qk, out_far, out_own,
    loc_sem, w_sem, l1_send, l1_recv, m1_send, m1_recv, l2_send, l2_recv, m2_send, m2_recv,
    sq_sem, o_send, o_recv,
):
    g = lax.axis_index("group")
    s = lax.axis_index("seq")
    e = lax.axis_index("expert")
    z = g // ND
    d = g % ND
    p = d * 2 + s
    reqs = NZ * ND
    tokens = 256
    half = 128
    feats = emb_v.shape[1]
    chunks = w_hbm.shape[2] // CW
    width = w_hbm.shape[2]

    emb_cp = pltpu.make_async_copy(emb_hbm.at[0], emb_v, loc_sem.at[0])
    tab_cp = pltpu.make_async_copy(tab_hbm, tab_v, loc_sem.at[1])
    small = [
        pltpu.make_async_copy(src, dst, loc_sem.at[3 + k])
        for k, (src, dst) in enumerate([
            (lat_hbm, lat_ref), (order_hbm, order_s), (time_hbm, time_s), (len_hbm, len_s), (gain_hbm, gain_ref)])
    ]
    for cp in small[:4]:
        cp.start()
    tab_cp.start()
    emb_cp.start()
    small[4].start()

    def w_copy(i):
        return pltpu.make_async_copy(
            w_hbm.at[i // chunks, :, pl.ds(pl.multiple_of((i % chunks) * CW, CW), CW)],
            wbuf.at[i % SLOTS], w_sem.at[i],
        )

    def w_start(i, c):
        w_copy(i).start()
        return c


    barrier = pltpu.get_barrier_semaphore()

    def greet_z(k, c):
        pl.semaphore_signal(barrier, inc=1, device_id={"group": ((z + k) % NZ) * ND + d}, device_id_type=MESH)
        return c

    def greet_p(k, c):
        q = (p + k) % (2 * ND)
        pl.semaphore_signal(barrier, inc=1, device_id={"group": z * ND + q // 2, "seq": q % 2}, device_id_type=MESH)
        return c

    lax.fori_loop(1, NZ, greet_z, 0)
    lax.fori_loop(1, 2 * ND, greet_p, 0)
    lax.fori_loop(0, SLOTS, w_start, 0)

    small[0].wait()

    def l1_copy(k, slot):
        return pltpu.make_async_remote_copy(
            src_ref=lat_ref.at[0], dst_ref=lat_all.at[slot], send_sem=l1_send.at[k], recv_sem=l1_recv.at[slot],
            device_id={"group": ((z + k) % NZ) * ND + d}, device_id_type=MESH)

    def l1_start(k, c):
        l1_copy(k, z).start()
        return c

    lat_all[z] = lat_ref[0]

    for cp in small[1:4]:
        cp.wait()

    rows = lax.broadcasted_iota(jnp.int32, (reqs, 128), 0)

    def pick(r, c):
        col, stamp, live = c
        where = order_s[r]
        col = jnp.where(rows == where, time_s[r], col)
        mine = where == g
        return col, jnp.where(mine, time_s[r], stamp), jnp.where(mine, len_s[r], live)

    col, stamp, live = lax.fori_loop(
        0, reqs, pick, (jnp.zeros((reqs, 128), jnp.int32), jnp.int32(0), jnp.int32(0)), unroll=8)
    expert_of = jnp.where(stamp >= bound_s[0], 0, 1)
    shown = jnp.where(expert_of == e, live, 0)

    steps = tab_v.shape[1]
    tab_cp.wait()
    hit = jnp.where(lax.broadcasted_iota(jnp.int32, (reqs, steps), 1) == col[:, :1], 1.0, 0.0).astype(BF16)

    def picked_of(part):
        return lax.dot_general(hit, part, (((1,), (1,)), ((), ())), preferred_element_type=F32)

    part_a = tab_v[...].astype(BF16)
    rest = tab_v[...] - part_a.astype(F32)
    part_b = rest.astype(BF16)
    part_c = (rest - part_b.astype(F32)).astype(BF16)
    picked = picked_of(part_a) + (picked_of(part_b) + picked_of(part_c))
    mod_src[...] = jnp.zeros_like(mod_src)
    for a in range(NZ):
        mod_src[a, :, : tab_v.shape[0]] = picked[a * ND : (a + 1) * ND]

    pl.semaphore_wait(barrier, NZ - 1 + 2 * ND - 1)
    lax.fori_loop(1, NZ, l1_start, 0, unroll=True)

    def m1_copy(k, slot):
        z2 = (z + k) % NZ
        return pltpu.make_async_remote_copy(
            src_ref=mod_src.at[z2], dst_ref=mod_all.at[slot], send_sem=m1_send.at[k], recv_sem=m1_recv.at[slot],
            device_id={"group": z2 * ND + d}, device_id_type=MESH)

    def m1_start(k, c):
        m1_copy(k, z).start()
        return c

    lax.fori_loop(1, NZ, m1_start, 0, unroll=True)
    mod_all[z] = mod_src[z]

    def l1_wait(k, c):
        l1_copy(k, (z + k) % NZ).wait_recv()
        return c

    lax.fori_loop(1, NZ, l1_wait, 0)
    for b in range(ND):
        chosen = jnp.zeros(lat_all.shape[1:], BF16)
        for a in range(NZ):
            chosen = jnp.where(order_s[a * ND + d] == z * ND + b, lat_all[a], chosen)
        lat_send[b] = chosen

    def l2_copy(k, slot):
        q = (p + k) % (2 * ND)
        return pltpu.make_async_remote_copy(
            src_ref=lat_send.at[q // 2], dst_ref=lat_recv.at[slot], send_sem=l2_send.at[k], recv_sem=l2_recv.at[slot],
            device_id={"group": z * ND + q // 2, "seq": q % 2}, device_id_type=MESH)

    def l2_start(k, c):
        l2_copy(k, p).start()
        return c

    lax.fori_loop(1, 2 * ND, l2_start, 0, unroll=5)
    lat_recv[p] = lat_send[d]

    def m1_wait(k, c):
        m1_copy(k, (z + k) % NZ).wait_recv()
        return c

    lax.fori_loop(1, NZ, m1_wait, 0)
    for b in range(ND):
        for a in range(NZ):
            mod_send[b, a : a + 1] = mod_all[a, b : b + 1]

    def m2_copy(k, slot):
        q = (p + k) % (2 * ND)
        return pltpu.make_async_remote_copy(
            src_ref=mod_send.at[q // 2], dst_ref=mod_recv.at[slot], send_sem=m2_send.at[k], recv_sem=m2_recv.at[slot],
            device_id={"group": z * ND + q // 2, "seq": q % 2}, device_id_type=MESH)

    def m2_start(k, c):
        m2_copy(k, p).start()
        return c

    lax.fori_loop(1, 2 * ND, m2_start, 0, unroll=5)
    mod_recv[p] = mod_send[d]

    emb_cp.wait()
    wbar = jnp.sum(emb_v[...].astype(F32), axis=1, keepdims=True) * (1.0 / feats)
    et = 256
    tiles = feats // et

    def gram_step(i, gram):
        centred = emb_v[:, pl.ds(pl.multiple_of(i * et, et), et)].astype(F32) - wbar
        return gram + lax.dot_general(
            centred, centred, (((1,), (1,)), ((), ())), precision=HI, preferred_element_type=F32)

    patch = emb_v.shape[0]
    gram = lax.fori_loop(0, tiles, gram_step, jnp.zeros((patch, patch), F32), unroll=4) * (1.0 / feats)
    right = jnp.concatenate([jnp.broadcast_to(wbar, (patch, 128)), gram, jnp.zeros((patch, 128 - patch), F32)], axis=1)
    for k in range(3):
        part = right.astype(BF16)
        right_v[k] = part
        right = right - part.astype(F32)

    def l2_wait(k, c):
        l2_copy(k, (p + k) % (2 * ND)).wait_recv()
        return c

    lax.fori_loop(1, 2 * ND, l2_wait, 0)
    for t in range(2):
        x = lat_recv[t].astype(F32)
        for b in range(1, ND):
            x = x + lat_recv[2 * b + t].astype(F32)
        xt[t * half : (t + 1) * half] = jnp.transpose(x).astype(BF16)

    xb = xt[...]
    both = [jnp.dot(xb, right_v[k], preferred_element_type=F32) for k in range(3)]
    both = both[0] + (both[1] + both[2])
    mean = both[:, :128]
    var = jnp.sum(both[:, 128 : 128 + patch] * xb.astype(F32), axis=1, keepdims=True)
    rstd = jnp.broadcast_to(1.0 / jnp.sqrt(jnp.maximum(var, 0.0) + EPS), (tokens, 128))

    def m2_wait(k, c):
        m2_copy(k, (p + k) % (2 * ND)).wait_recv()
        return c

    lax.fori_loop(1, 2 * ND, m2_wait, 0)
    own = tab_v.shape[0] // 2
    lane = lax.broadcasted_iota(jnp.int32, (NZ, 128), 1)
    span = 2 * ND * own // 128
    for c in range(2):
        pieces = [jnp.zeros((NZ, 128), F32) for _ in range(span)]
        for q in range(2 * ND):
            start = q * own
            off = start % 128
            turned = pltpu.roll(mod_recv[q], (off - c * own) % 128, 1)
            a = start // 128
            pieces[a] = jnp.where((lane >= off) & (lane < off + own), turned, pieces[a])
            if off + own > 128:
                pieces[a + 1] = jnp.where(lane < off + own - 128, turned, pieces[a + 1])
        for a in range(span):
            for b in range(NZ):
                n = (b * span + a) * 128
                mod_row[c : c + 1, n : n + 128] = pieces[a][b : b + 1] + float(c)

    def arrive(i, c):
        w_copy(i).wait()
        return c

    lax.fori_loop(0, chunks, arrive, 0)

    def modulate(i, c):
        tile = pl.ds(pl.multiple_of(i * et, et), et)
        for t in range(2):
            rows_t = slice(t * half, (t + 1) * half)
            made = jnp.dot(xt[rows_t], emb_v[:, tile], preferred_element_type=F32)
            for h in range(et // 128):
                cols = pl.ds(pl.multiple_of(i * et + h * 128, 128), 128)
                v = (made[:, h * 128 : (h + 1) * 128] - mean[rows_t]) * rstd[rows_t]
                normed[rows_t, cols] = (v * mod_row[1:2, cols] + mod_row[0:1, cols]).astype(BF16)
        return c

    lax.fori_loop(0, tiles, modulate, 0, unroll=NORM)

    def project(i):
        return jnp.dot(normed[...], wbuf[i % SLOTS], preferred_element_type=F32)

    def squares(base):
        def body(i, ss):
            made = project(base + i)
            proj[base + i] = made
            made = made * made
            return ss + (made[:, :128] + made[:, 128:])
        return lax.fori_loop(0, chunks, body, jnp.zeros((tokens, 128), F32), unroll=UNROLL)

    ones = jnp.ones((8, 128), F32)

    def as_rows(ss):
        return lax.dot_general(ones, ss, (((1,), (1,)), ((), ())), precision=HI, preferred_element_type=F32)

    q_ss = squares(0)
    lax.fori_loop(SLOTS, 3 * chunks, w_start, 0)
    lax.fori_loop(chunks, 2 * chunks, arrive, 0)
    k_ss = squares(chunks)
    sq_send[0] = as_rows(q_ss)
    sq_send[1] = as_rows(k_ss)
    sq_cp = pltpu.make_async_remote_copy(
        src_ref=sq_send, dst_ref=sq_recv, send_sem=sq_sem.at[0], recv_sem=sq_sem.at[1],
        device_id={"seq": 1 - s}, device_id_type=MESH)
    sq_cp.start()

    def values(i, c):
        vbuf[i] = project(2 * chunks + i).astype(BF16)
        return c

    first = chunks // 2
    lax.fori_loop(2 * chunks, 3 * chunks, arrive, 0)
    small[4].wait()
    lax.fori_loop(0, first, values, 0, unroll=first)
    sq_cp.wait_recv()
    for c in range(2):
        total = sq_send[c] + sq_recv[c]
        inv = 1.0 / jnp.sqrt(total * (1.0 / (2 * width)) + EPS)
        inv = jnp.broadcast_to(inv[0:1], (128, tokens))
        inv_qk[c] = jnp.transpose(inv)

    keypos = lax.broadcasted_iota(jnp.int32, (half, tokens), 1)
    rowpos = lax.broadcasted_iota(jnp.int32, (half, HD), 0)

    def o_copy(i, side):
        cols = pl.ds(pl.multiple_of(i * CW, CW), CW)
        there = pl.ds(pl.multiple_of(side * width + i * CW, CW), CW)
        return pltpu.make_async_remote_copy(
            src_ref=out_far.at[:, cols], dst_ref=out_hbm.at[0, :, there], send_sem=o_send.at[i], recv_sem=o_recv.at[i],
            device_id={"seq": 1 - s}, device_id_type=MESH)

    def attend(i, r0, out_ref, first):
        at = pl.ds(pl.multiple_of(r0, half), half)
        work = []
        for u in range(PAIRS):
            n = i * PAIRS + u
            for j in range(CW // HD):
                hc = slice(j * HD, (j + 1) * HD)
                cols = pl.ds(pl.multiple_of(n * CW + j * HD, HD), HD)
                if first:
                    kbuf[n, :, hc] = (proj[chunks + n, :, hc] * inv_qk[1] * gain_ref[0, 1:2, cols]).astype(BF16)
                qn = (proj[n, at, hc] * inv_qk[0, at, :] * gain_ref[0, 0:1, cols]).astype(BF16)
                work.append((n, hc, cols, qn))
        scores = [lax.dot_general(qn, kbuf[n, :, hc], (((1,), (1,)), ((), ())), preferred_element_type=F32)
                  for n, hc, _, qn in work]
        parts = []
        for sc in scores:
            sc = jnp.where(keypos < live, sc * HD ** (-0.5), -jnp.inf)
            ex = jnp.exp(sc - jnp.max(sc, axis=1, keepdims=True))
            parts.append((ex * (1.0 / jnp.sum(ex, axis=1, keepdims=True))).astype(BF16))
        for k, ((n, hc, cols, _), pr) in enumerate(zip(work, parts)):
            mixed = jnp.dot(pr, vbuf[n, :, hc], preferred_element_type=F32)
            out_ref[:, cols] = jnp.where(rowpos + r0 < shown, mixed, 0.0).astype(BF16)
            if first and k % 2 == 1:
                o_copy(n, s).start()

    def far(i, c):
        attend(i, (1 - s) * half, out_far, True)
        return c

    far(0, 0)
    lax.fori_loop(first, chunks, values, 0, unroll=first)
    far(1, 0)

    def near(i, c):
        attend(i, s * half, out_own, False)
        return c

    near(0, 0)
    near(1, 0)
    own_cp = pltpu.make_async_copy(
        out_own, out_hbm.at[0, :, pl.ds(pl.multiple_of(s * width, width), width)], loc_sem.at[2])
    own_cp.start()

    def sends_z(k, c):
        l1_copy(k, z).wait_send()
        m1_copy(k, z).wait_send()
        return c

    def sends_p(k, c):
        l2_copy(k, p).wait_send()
        m2_copy(k, p).wait_send()
        return c

    lax.fori_loop(1, NZ, sends_z, 0)
    lax.fori_loop(1, 2 * ND, sends_p, 0)

    def o_wait(i, c):
        o_copy(i, 1 - s).wait_recv()
        o_copy(i, s).wait_send()
        return c

    sq_cp.wait_send()
    lax.fori_loop(0, chunks, o_wait, 0)
    own_cp.wait()


def per_device(latents, timestep, boundary, order, lengths, embed_weight, mod_table, qkv_weight, qk_gain):
    patch, feats = embed_weight.shape[1:]
    width = qkv_weight.shape[3]
    chunks = width // CW
    steps = mod_table.shape[1]
    table = jnp.transpose(mod_table[0], (1, 2, 0)).reshape(-1, steps)
    weights = jnp.transpose(qkv_weight[0], (1, 0, 2))
    tokens, half = 256, 128
    keep = functools.partial(pltpu.with_memory_space_constraint, memory_space=pltpu.HBM)
    smem = pl.BlockSpec(memory_space=pltpu.SMEM)
    hbm = pl.BlockSpec(memory_space=pltpu.HBM)
    anywhere = pl.BlockSpec(memory_space=pl.ANY)
    dma = pltpu.SemaphoreType.DMA
    return pl.pallas_call(
        kernel,
        out_shape=jax.ShapeDtypeStruct((1, half, 2 * width), BF16),
        in_specs=[hbm] * 2 + [smem] + [hbm] * 6,
        out_specs=anywhere,
        scratch_shapes=[
            pltpu.SMEM(order.shape, jnp.int32),
            pltpu.SMEM(timestep.shape, jnp.int32),
            pltpu.SMEM(lengths.shape, jnp.int32),
            pltpu.VMEM(latents.shape, BF16),
            pltpu.VMEM(qk_gain.shape, F32),
            pltpu.VMEM((patch, feats), BF16),
            pltpu.VMEM(table.shape, F32),
            pltpu.VMEM((SLOTS, feats, CW), BF16),
            pltpu.VMEM((NZ, patch, half), BF16),
            pltpu.VMEM((ND, patch, half), BF16),
            pltpu.VMEM((2 * ND, patch, half), BF16),
            pltpu.VMEM((NZ, ND, 128), F32),
            pltpu.VMEM((NZ, ND, 128), F32),
            pltpu.VMEM((ND, NZ, 128), F32),
            pltpu.VMEM((2 * ND, NZ, 128), F32),
            pltpu.VMEM((2, feats), F32),
            pltpu.VMEM((3, patch, 256), BF16),
            pltpu.VMEM((tokens, patch), BF16),
            pltpu.VMEM((tokens, feats), BF16),
            pltpu.VMEM((2 * chunks, tokens, CW), F32),
            pltpu.VMEM((chunks, tokens, CW), BF16),
            pltpu.VMEM((chunks, tokens, CW), BF16),
            pltpu.VMEM((2, 8, tokens), F32),
            pltpu.VMEM((2, 8, tokens), F32),
            pltpu.VMEM((2, tokens, 128), F32),
            pltpu.VMEM((half, width), BF16),
            pltpu.VMEM((half, width), BF16),
            dma((8,)),
            dma((3 * chunks,)),
            dma((NZ,)), dma((NZ,)), dma((NZ,)), dma((NZ,)),
            dma((2 * ND,)), dma((2 * ND,)), dma((2 * ND,)), dma((2 * ND,)),
            dma((2,)),
            dma((chunks,)), dma((chunks,)),
        ],
        compiler_params=pltpu.CompilerParams(
            collective_id=0, has_side_effects=True, vmem_limit_bytes=48 * 1024 * 1024),
        cost_estimate=pl.CostEstimate(flops=13 * 10**9, bytes_accessed=49 * 10**6, transcendentals=800000),
    )(keep(order), keep(timestep), boundary, keep(lengths), keep(latents), keep(qk_gain), keep(embed_weight),
      keep(table), keep(weights))


def solution(mesh):
    in_specs = (
        P("group", None, "seq"),
        P(),
        P(),
        P(),
        P(),
        P("expert", None, None),
        P("expert", None, None, ("group", "seq")),
        P("expert", None, None, "seq"),
        P("expert", None, "seq"),
    )
    out_specs = P(("expert", "group"), "seq", None)
    return jax.shard_map(
        per_device, mesh=mesh, in_specs=in_specs, out_specs=out_specs, check_vma=False
    )
```
